128 devices in a mesh: section: 2 (over core), shard: 2 (over z_hi), replica: 32 (over y, z_lo, x).
Axes of the slice: x: 4, y: 4, z: 4 (z_hi: 2, z_lo: 2; z = z_hi * 2 + z_lo), core: 2. Of those that a mesh axis runs over, the one named last changes fastest.
Arguments:
- layer_input: bfloat16 [128, 128, 1152], P('replica'), may hold values from -6 to 6
- cotangent: bfloat16 [128, 128, 1152], P('replica'), may hold values from -6 to 6
- attn_gain: float32 [2, 1152], P('section'), may hold values from 0.5 to 1.5
- query_weight: bfloat16 [2, 1152, 1152], P('section', None, 'shard'), may hold values from -0.1875 to 0.1875
- key_matrix: bfloat16 [2, 1152, 384], P('section', None, 'shard'), may hold values from -0.1875 to 0.1875
- value_matrix: bfloat16 [2, 1152, 384], P('section', None, 'shard'), may hold values from -0.1875 to 0.1875
- output_weight: bfloat16 [2, 1152, 1152], P('section', 'shard'), may hold values from -0.75 to 0.75
- ffn_gain: float32 [2, 1152], P('section'), may hold values from 0.5 to 1.5
- gate_weight: bfloat16 [2, 1152, 3072], P('section', None, 'shard'), may hold values from -0.1875 to 0.1875
- up_weight: bfloat16 [2, 1152, 3072], P('section', None, 'shard'), may hold values from -0.1875 to 0.1875
- down_weight: bfloat16 [2, 3072, 1152], P('section', 'shard'), may hold values from -0.109375 to 0.109375
Outputs:
- activations: bfloat16 [2, 128, 128, 1152], P('section', 'replica')
- input_grads: bfloat16 [2, 128, 128, 1152], P('section', 'replica')
- attn_gain_grad: float32 [2, 1152], P('section', 'replica')
- query_grad: float32 [2, 1152, 1152], P('section', 'replica', 'shard')
- key_grad: float32 [2, 1152, 384], P('section', 'replica', 'shard')
- value_grad: float32 [2, 1152, 384], P('section', 'replica', 'shard')
- output_grad: float32 [2, 1152, 1152], P('section', 'shard', 'replica')
- ffn_gain_grad: float32 [2, 1152], P('section', 'replica')
- gate_grad: float32 [2, 1152, 3072], P('section', 'replica', 'shard')
- up_grad: float32 [2, 1152, 3072], P('section', 'replica', 'shard')
- down_grad: float32 [2, 3072, 1152], P('section', 'shard', 'replica')
The draws below stay inside these ranges and needn't reach their ends.
All inputs are finite; a program needn't handle non-finite values.
Results may differ from the reference program's by a relative error of at most 0.03.
Values may be sent and summed in bfloat16 or wider, within the bound.
A program may use at most 256 MiB of HBM per device.

```python
import jax
import jax.numpy as jnp
from jax import lax

MODEL_WIDTH = 1152
QUERY_HEADS = 18
KEY_VALUE_HEADS = 6
HEAD_SIZE = 64
FF = 3072
LEN = 128
SEQS = 128
N_SECTION = 2


def steps_of(own_key, shape, split, least, largest):
    level = 1.0
    for axis_at, shards_of in split:
        steps = jax.random.uniform(jax.random.fold_in(jax.random.fold_in(own_key, 6), axis_at), (shards_of,), jnp.float32, least / len(split), largest / len(split))
        level = level * jnp.repeat(jnp.exp(steps), shape[axis_at] // shards_of).reshape((-1,) + (1,) * (len(shape) - 1 - axis_at))
    return level


def bell_draw(stream_key, dims, width, limit, cuts=(), kind=jnp.bfloat16):
    entries = width * jax.random.normal(stream_key, dims, jnp.float32)
    if cuts:
        entries = entries * steps_of(stream_key, dims, cuts, -0.22, 0.18)
    return jnp.clip(entries, -limit, limit).astype(kind)


def setup_inputs(seed: int = 0) -> dict:
    streams_of = jax.random.split(jax.random.key(seed), 12)
    return {
        "layer_input": bell_draw(streams_of[0], (SEQS, LEN, MODEL_WIDTH), 1.0, 6.0, ((0, 32),)),
        "cotangent": bell_draw(streams_of[1], (SEQS, LEN, MODEL_WIDTH), 1.0, 6.0, ((0, 32),)),
        "attn_gain": jnp.clip(1.0 + 0.1 * jax.random.normal(streams_of[2], (N_SECTION, MODEL_WIDTH), jnp.float32), 0.5, 1.5),
        "query_weight": bell_draw(streams_of[3], (N_SECTION, MODEL_WIDTH, QUERY_HEADS * HEAD_SIZE), MODEL_WIDTH ** -0.5, 0.1875, ((0, 2), (2, 2))),
        "key_matrix": bell_draw(streams_of[4], (N_SECTION, MODEL_WIDTH, KEY_VALUE_HEADS * HEAD_SIZE), MODEL_WIDTH ** -0.5, 0.1875, ((0, 2), (2, 2))),
        "value_matrix": bell_draw(streams_of[5], (N_SECTION, MODEL_WIDTH, KEY_VALUE_HEADS * HEAD_SIZE), MODEL_WIDTH ** -0.5, 0.1875, ((0, 2), (2, 2))),
        "output_weight": bell_draw(streams_of[6], (N_SECTION, QUERY_HEADS * HEAD_SIZE, MODEL_WIDTH), (QUERY_HEADS * HEAD_SIZE // 16) ** -0.5, 0.75, ((0, 2), (1, 2))),
        "ffn_gain": jnp.clip(1.0 + 0.1 * jax.random.normal(streams_of[7], (N_SECTION, MODEL_WIDTH), jnp.float32), 0.5, 1.5),
        "gate_weight": bell_draw(streams_of[8], (N_SECTION, MODEL_WIDTH, FF), MODEL_WIDTH ** -0.5, 0.1875, ((0, 2), (2, 2))),
        "up_weight": bell_draw(streams_of[9], (N_SECTION, MODEL_WIDTH, FF), MODEL_WIDTH ** -0.5, 0.1875, ((0, 2), (2, 2))),
        "down_weight": bell_draw(streams_of[10], (N_SECTION, FF, MODEL_WIDTH), FF ** -0.5, 0.109375, ((0, 2), (1, 2))),
    }


EPSILON = 1e-05
ROPE_BASE = 10000.0

@jax.custom_vjp
def lower_precision(v):
    return lax.optimization_barrier(v.astype(jnp.bfloat16)).astype(jnp.float32)

@jax.custom_vjp
def lower_precision_back(v):
    return v

def low_keep(v):
    return (lower_precision(v), None)

def low_pass(kept, grad):
    return (grad,)

def back_keep(v):
    return (v, None)

def back_low(kept, grad):
    return (lower_precision(grad),)
lower_precision.defvjp(low_keep, low_pass)
lower_precision_back.defvjp(back_keep, back_low)

def rope_tables(sequence_length, head_size):
    half_size = head_size // 2
    position = jnp.arange(sequence_length, dtype=jnp.float32)
    frequency = ROPE_BASE ** (-jnp.arange(half_size, dtype=jnp.float32) * 2.0 / head_size)
    angles = position[:, None] * frequency[None, :]
    return (jnp.cos(angles), jnp.sin(angles))

def rotary_apply(heads, cosine_lookup, sine_lookup):
    half_size = heads.shape[-1] // 2
    first_half = heads[..., :half_size]
    second_half = heads[..., half_size:]
    cosine_part = cosine_lookup[:, None, :]
    sine_part = sine_lookup[:, None, :]
    return jnp.concatenate([first_half * cosine_part - second_half * sine_part, second_half * cosine_part + first_half * sine_part], -1)

def norm_scale(value_rows):
    return lax.rsqrt(lax.optimization_barrier(jnp.mean(value_rows * value_rows, axis=-1, keepdims=True)) + EPSILON)

def matrix_product(left, right):
    return jnp.einsum('bld,df->blf', left, right, precision=lax.Precision.HIGHEST)

def block(hidden_in, gain_attn, weight_q, key_weight_param, value_weight_param, weight_o, gain_ffn, weight_gate, weight_up, weight_down):
    sequence_count, sequence_length, feature_count = hidden_in.shape
    cosine_lookup, sine_lookup = rope_tables(sequence_length, HEAD_SIZE)
    group_count = QUERY_HEADS // KEY_VALUE_HEADS
    normalized_rows = lower_precision(hidden_in * norm_scale(hidden_in) * gain_attn)
    query_rows = lower_precision(rotary_apply(lower_precision_back(matrix_product(normalized_rows, weight_q)).reshape(sequence_count, sequence_length, QUERY_HEADS, HEAD_SIZE), cosine_lookup, sine_lookup))
    key_head_rows = lower_precision(rotary_apply(lower_precision_back(matrix_product(normalized_rows, key_weight_param)).reshape(sequence_count, sequence_length, KEY_VALUE_HEADS, HEAD_SIZE), cosine_lookup, sine_lookup))
    value_rows = lower_precision(lower_precision_back(matrix_product(normalized_rows, value_weight_param))).reshape(sequence_count, sequence_length, KEY_VALUE_HEADS, HEAD_SIZE)
    grouped_heads = query_rows.reshape(sequence_count, sequence_length, KEY_VALUE_HEADS, group_count, HEAD_SIZE)
    scores = lower_precision_back(jnp.einsum('blkgd,bmkd->bkglm', grouped_heads, key_head_rows, precision=lax.Precision.HIGHEST) * HEAD_SIZE ** (-0.5))
    causal = jnp.arange(sequence_length)[:, None] >= jnp.arange(sequence_length)[None, :]
    scores = jnp.where(causal, scores, -1e+30)
    probabilities = jax.nn.softmax(scores, axis=-1)
    mixed_heads = jnp.einsum('bkglm,bmkd->blkgd', lower_precision(probabilities), value_rows, precision=lax.Precision.HIGHEST)
    mixed_heads = lower_precision(lower_precision_back(mixed_heads)).reshape(sequence_count, sequence_length, QUERY_HEADS * HEAD_SIZE)
    middle = hidden_in + lower_precision_back(matrix_product(mixed_heads, weight_o))
    ffn_in = lower_precision(middle * norm_scale(middle) * gain_ffn)
    gate_pre = lower_precision_back(matrix_product(ffn_in, weight_gate))
    up_pre = lower_precision_back(matrix_product(ffn_in, weight_up))
    hidden = lower_precision(jax.nn.silu(gate_pre) * up_pre)
    return middle + lower_precision_back(matrix_product(hidden, weight_down))

def reference(layer_input, cotangent, attn_gain, query_weight, key_matrix, value_matrix, output_weight, ffn_gain, gate_weight, up_weight, down_weight):
    weights = tuple((item_array.astype(jnp.float32) for item_array in (attn_gain, query_weight, key_matrix, value_matrix, output_weight, ffn_gain, gate_weight, up_weight, down_weight)))
    start_rows = layer_input.astype(jnp.float32)
    cotangent_rows = cotangent.astype(jnp.float32)

    def forward(start_rows, deltas, weights):
        current = start_rows
        results = []
        for depth_index in range(N_SECTION):
            if depth_index > 0:
                current = lower_precision_back(lower_precision(current)) + deltas[depth_index - 1]
            current = block(current, *[item_array[depth_index] for item_array in weights])
            results.append(current)
        return (current, jnp.stack(results))
    deltas = tuple((jnp.zeros_like(start_rows) for depth_index in range(N_SECTION - 1)))
    final_rows, pull_back, stacked = jax.vjp(forward, start_rows, deltas, weights, has_aux=True)
    start_grad, delta_grads, weight_grads = pull_back(cotangent_rows)
    activations = stacked.astype(jnp.bfloat16)
    input_grads = jnp.stack((start_grad,) + tuple(delta_grads)).astype(jnp.bfloat16)
    return (activations, input_grads, weight_grads[0], weight_grads[1], weight_grads[2], weight_grads[3], weight_grads[4], weight_grads[5], weight_grads[6], weight_grads[7], weight_grads[8])
```

```python
import functools

import jax
import jax.numpy as jnp
import numpy as np
from jax import lax
from jax.experimental import pallas as pl
from jax.experimental.pallas import tpu as pltpu
from jax.sharding import PartitionSpec as P

HEAD = 64
HEADS = 9
GROUPS = 3
WIDTH = 1152
FF = 1536
LEN = 128
SEQS = 4
TOKENS = LEN * SEQS
QW = HEADS * HEAD
KW = GROUPS * HEAD
RING = 4
PIECE = 80
ROWS = RING * RING * PIECE
OWN = WIDTH // 32
EPSILON = 1e-05
ROPE_BASE = 10000.0
F32 = jnp.float32
BF16 = jnp.bfloat16
MESH = pl.DeviceIdType.MESH
PART_DOWN, PART_GATE, PART_UP, PART_MIX = 0, 1, 2, 3
PARTS = ((1536, "x"), (1536, "y"), (1536, "y"), (1664, "x"))
BLOCKS = (
    (0, 0, 768, 384),
    (1, 0, 768, 384),
    (0, 768, 768, 384),
    (1, 768, 768, 384),
    (3, 0, 768, 384),
    (2, 0, 768, 384),
    (3, 768, 896, 512),
    (2, 768, 768, 384),
)


def dot(left, right):
    return lax.dot_general(left, right, (((1,), (0,)), ((), ())), preferred_element_type=F32)


def dot_nt(left, right):
    return lax.dot_general(left, right, (((1,), (1,)), ((), ())), preferred_element_type=F32)


def dot_tn(left, right):
    return lax.dot_general(left, right, (((0,), (0,)), ((), ())), preferred_element_type=F32)


def rope_tables():
    half = HEAD // 2
    position = np.arange(LEN, dtype=np.float32)
    frequency = (ROPE_BASE ** (-np.arange(half, dtype=np.float32) * 2.0 / HEAD)).astype(np.float32)
    angles = position[:, None] * frequency[None, :]
    cosine = np.cos(angles).astype(np.float32)
    sine = np.sin(angles).astype(np.float32)
    return (
        np.tile(np.concatenate([cosine, cosine], 1), (1, HEADS)),
        np.tile(np.concatenate([sine, sine], 1), (1, HEADS)),
    )


def turn_matrix():
    turn = np.zeros((QW, QW), np.float32)
    for head in range(HEADS):
        for j in range(HEAD // 2):
            first, second = head * HEAD + j, head * HEAD + HEAD // 2 + j
            turn[second, first] = -1.0
            turn[first, second] = 1.0
    return turn


def place_matrix():
    place = np.zeros((RING, RING, PIECE, WIDTH), np.float32)
    for y in range(RING):
        for x in range(RING):
            for z in range(2):
                owner = (y * 2 + z) * RING + x
                for i in range(OWN):
                    place[y, x, z * 40 + i, owner * OWN + i] = 1.0
    return place.reshape(ROWS, WIDTH)


def rms_factor(rows):
    return lax.rsqrt(jnp.mean(rows * rows, axis=-1, keepdims=True) + EPSILON)


def norm_back(rows, factor, grad):
    return factor * grad - rows * factor**3 * jnp.mean(grad * rows, axis=-1, keepdims=True)


def sequence(m):
    return pl.ds(pl.multiple_of(m * LEN, LEN), LEN)


def compute_kernel(
    x_ref, cot_ref, ga_ref, wq_ref, wk_ref, wv_ref, wo_ref, gf_ref, wg_ref, wu_ref, wd_ref,
    cos_ref, sin_ref, turn_ref, place_ref,
    act_ref, ig_ref, g0_ref, g1_ref, g2_ref, g3_ref,
    wqr, wkr, hin, gin, normed, qs, qr, ks, kr, vs, probs, mixed, middle, ffn_in, gates, ups, hidden,
    attn_in, qkv_back, gain_acc, xt, snd, rcv, act_stage, ig_stage, g_stage,
    in_sem, in_send, hin_sem, gin_sem, ar_send, ar_recv, step_send, out_sem, out_send, g_sem,
):
    section = lax.axis_index("section")
    shard = lax.axis_index("shard")
    rep = lax.axis_index("replica")
    zlo = lax.rem(lax.div(rep, RING), 2)
    side = rep + RING - 2 * RING * zlo
    core = {"section": 1 - section}
    twin = {"shard": 1 - shard, "replica": side}
    swap = {"replica": side}

    barrier = pltpu.get_barrier_semaphore()
    for target in (core, twin, swap):
        pl.semaphore_signal(barrier, inc=1, device_id=target, device_id_type=MESH)
    pl.semaphore_wait(barrier, 3)

    def fetch(source, target, sem, m):
        rows = sequence(m)

        def local():
            return pltpu.make_async_copy(source.at[m], target.at[rows], sem.at[m])

        def push():
            return pltpu.make_async_remote_copy(
                source.at[m], target.at[rows], in_send.at[m], sem.at[m],
                device_id=swap, device_id_type=MESH,
            )

        return local, push

    for m in range(SEQS):
        for s, (source, target, sem) in enumerate(((x_ref, hin, hin_sem), (cot_ref, gin, gin_sem))):
            local, push = fetch(source, target, sem, m)

            @pl.when((section == s) & (shard == 0))
            def _():
                local().start()

            @pl.when((section == s) & (shard == 1))
            def _():
                push().start()

    def wait_rows(source, target, sem, m, s):
        local, push = fetch(source, target, sem, m)

        @pl.when((section == s) & (shard == 0))
        def _():
            local().wait()

        @pl.when((section == s) & (shard == 1))
        def _():
            push().wait_recv()

    def pass_on(stage, target, sem, m, which):
        rows = sequence(m)
        return pltpu.make_async_remote_copy(
            stage.at[rows], target.at[rows], step_send.at[which, m], sem.at[m],
            device_id=core, device_id_type=MESH,
        )

    def exchange(phase, m):
        rows = sequence(m)
        return pltpu.make_async_remote_copy(
            snd.at[phase, rows], rcv.at[phase, rows], ar_send.at[phase, m], ar_recv.at[phase, m],
            device_id=twin, device_id_type=MESH,
        )

    def exchanged(phase, m):
        exchange(phase, m).wait_recv()
        rows = sequence(m)
        return snd[phase, rows, :].astype(F32) + rcv[phase, rows, :].astype(F32)

    def emit(stage, target, which, m):
        rows = sequence(m)

        def local():
            return pltpu.make_async_copy(stage.at[rows], target.at[m], out_sem.at[which, m])

        def push():
            return pltpu.make_async_remote_copy(
                stage.at[rows], target.at[m], out_send.at[which, m], out_sem.at[which, m],
                device_id=swap, device_id_type=MESH,
            )

        return local, push

    def start_emit(stage, target, which, m):
        local, push = emit(stage, target, which, m)

        @pl.when(shard == 0)
        def _():
            local().start()

        @pl.when(shard == 1)
        def _():
            push().start()

    turn = turn_ref[...]
    wqr[...] = dot(wq_ref[...], turn).astype(BF16)
    wkr[...] = dot(wk_ref[...], turn[:KW, :KW]).astype(BF16)
    gain_acc[...] = jnp.zeros_like(gain_acc)
    mixed[:, QW:] = jnp.zeros((TOKENS, 64), BF16)
    qkv_back[:, QW + 2 * KW:] = jnp.zeros((TOKENS, 64), BF16)

    def stacked(value, g):
        return jnp.concatenate(
            [value[:, (3 * g + j) * HEAD:(3 * g + j + 1) * HEAD] for j in range(3)], axis=0
        )

    def attention(m):
        rows = sequence(m)
        wait_rows(x_ref, hin, hin_sem, m, 0)

        @pl.when(section == 1)
        def _():
            pass_on(act_stage, hin, hin_sem, m, 0).wait_recv()

        h = hin[rows, :].astype(F32)
        normal = (h * rms_factor(h) * ga_ref[...]).astype(BF16)
        normed[rows, :] = normal
        cosine, sine = cos_ref[...], sin_ref[...]
        query = (dot(normal, wq_ref[...]) * cosine + dot(normal, wqr[...]) * sine).astype(BF16)
        key = (
            dot(normal, wk_ref[...]) * cosine[:, :KW] + dot(normal, wkr[...]) * sine[:, :KW]
        ).astype(BF16)
        value = dot(normal, wv_ref[...]).astype(BF16)
        qs[rows, :] = query
        ks[rows, :] = key
        vs[rows, :] = value
        qr[rows, :] = dot(query, turn_ref[...]).astype(BF16)
        kr[rows, :] = dot(key, turn_ref[:KW, :KW]).astype(BF16)
        at = lax.rem(lax.broadcasted_iota(jnp.int32, (3 * LEN, LEN), 0), LEN)
        causal = at >= lax.broadcasted_iota(jnp.int32, (3 * LEN, LEN), 1)
        heads = []
        for g in range(GROUPS):
            cols = slice(g * HEAD, (g + 1) * HEAD)
            scores = dot_nt(stacked(query, g), key[:, cols]) * HEAD**-0.5
            scores = jnp.where(causal, scores, -1e30)
            top = jnp.max(scores, axis=-1, keepdims=True)
            weight = jnp.exp(scores - top)
            prob = (weight / jnp.sum(weight, axis=-1, keepdims=True)).astype(BF16)
            probs[m, g] = prob
            out = dot(prob, value[:, cols]).astype(BF16)
            heads += [out[j * LEN:(j + 1) * LEN] for j in range(3)]
        mix = jnp.concatenate(heads, axis=1)
        mixed[rows, :QW] = mix
        snd[0, rows, :] = dot(mix, wo_ref[...]).astype(BF16)
        exchange(0, m).start()

    def feed_forward(m):
        rows = sequence(m)
        mid = hin[rows, :].astype(F32) + exchanged(0, m)
        middle[rows, :] = mid
        normal = (mid * rms_factor(mid) * gf_ref[...]).astype(BF16)
        ffn_in[rows, :] = normal
        for j in range(0, FF, 512):
            cols = slice(j, j + 512)
            gate = dot(normal, wg_ref[:, cols])
            up = dot(normal, wu_ref[:, cols])
            gates[rows, cols] = gate.astype(BF16)
            ups[rows, cols] = up.astype(BF16)
            hidden[rows, cols] = (gate * jax.nn.sigmoid(gate) * up).astype(BF16)
        snd[1, rows, :] = dot(hidden[rows, :], wd_ref[...]).astype(BF16)
        exchange(1, m).start()

    def finish(m):
        rows = sequence(m)
        act_stage[rows, :] = (middle[rows, :] + exchanged(1, m)).astype(BF16)

        @pl.when(section == 0)
        def _():
            pass_on(act_stage, hin, hin_sem, m, 0).start()

        start_emit(act_stage, act_ref, 0, m)

    def forward_tick(i, carry):
        @pl.when(i < SEQS)
        def _():
            attention(i)

        @pl.when(i >= 2)
        def _():
            finish(i - 2)

        @pl.when((i >= 1) & (i <= SEQS))
        def _():
            feed_forward(i - 1)

        return carry

    lax.fori_loop(0, SEQS + 2, forward_tick, 0)

    def feed_forward_back(m):
        rows = sequence(m)
        wait_rows(cot_ref, gin, gin_sem, m, 1)

        @pl.when(section == 0)
        def _():
            pass_on(ig_stage, gin, gin_sem, m, 1).wait_recv()

        down_in = gin[rows, :]
        total = jnp.zeros((LEN, WIDTH), F32)
        for j in range(0, FF, 512):
            cols = slice(j, j + 512)
            back = dot_nt(down_in, wd_ref[cols, :])
            gate = gates[rows, cols].astype(F32)
            up = ups[rows, cols].astype(F32)
            sig = jax.nn.sigmoid(gate)
            gate_back = (back * up * sig * (1.0 + gate * (1.0 - sig))).astype(BF16)
            up_back = (back * gate * sig).astype(BF16)
            gates[rows, cols] = gate_back
            ups[rows, cols] = up_back
            total += dot_nt(gate_back, wg_ref[:, cols]) + dot_nt(up_back, wu_ref[:, cols])
        snd[2, rows, :] = total.astype(BF16)
        exchange(2, m).start()

    def attention_back(m):
        rows = sequence(m)
        back = exchanged(2, m)
        mid = middle[rows, :]
        factor = rms_factor(mid)
        gain_acc[0:1, :] += jnp.sum(back * mid * factor, axis=0, keepdims=True)
        mid_back = gin[rows, :].astype(F32) + norm_back(mid, factor, back * gf_ref[...])
        middle[rows, :] = mid_back
        low = mid_back.astype(BF16)
        attn_in[rows, :] = low
        mixed_back = dot_nt(low, wo_ref[...]).astype(BF16)
        query, key, value = qs[rows, :], ks[rows, :], vs[rows, :]
        query_turn, key_turn = qr[rows, :], kr[rows, :]
        cosine, sine = cos_ref[:, :HEAD], sin_ref[:, :HEAD]
        query_out, key_out, value_out = [], [], []
        for g in range(GROUPS):
            cols = slice(g * HEAD, (g + 1) * HEAD)
            prob = probs[m, g]
            prob_f = prob.astype(F32)
            out_back = stacked(mixed_back, g)
            value_out.append(dot_tn(prob, out_back).astype(BF16))
            prob_back = dot_nt(out_back, value[:, cols])
            score_back = (
                prob_f * (prob_back - jnp.sum(prob_back * prob_f, axis=-1, keepdims=True))
            ).astype(BF16)
            both = jnp.concatenate([key[:, cols], key_turn[:, cols]], axis=1)
            turned = dot(score_back, both) * HEAD**-0.5
            for j in range(3):
                one = turned[j * LEN:(j + 1) * LEN]
                query_out.append((one[:, :HEAD] * cosine - one[:, HEAD:] * sine).astype(BF16))
            both = jnp.concatenate([stacked(query, g), stacked(query_turn, g)], axis=1)
            one = dot_tn(score_back, both) * HEAD**-0.5
            key_out.append((one[:, :HEAD] * cosine - one[:, HEAD:] * sine).astype(BF16))
        query_back = jnp.concatenate(query_out, axis=1)
        key_back = jnp.concatenate(key_out, axis=1)
        value_back = jnp.concatenate(value_out, axis=1)
        qkv_back[rows, :QW + 2 * KW] = jnp.concatenate([query_back, key_back, value_back], axis=1)
        snd[3, rows, :] = (
            dot_nt(query_back, wq_ref[...])
            + dot_nt(key_back, wk_ref[...])
            + dot_nt(value_back, wv_ref[...])
        ).astype(BF16)
        exchange(3, m).start()

    def finish_back(m):
        rows = sequence(m)
        back = exchanged(3, m)
        h = hin[rows, :].astype(F32)
        factor = rms_factor(h)
        gain_acc[1:2, :] += jnp.sum(back * h * factor, axis=0, keepdims=True)
        ig_stage[rows, :] = (
            middle[rows, :] + norm_back(h, factor, back * ga_ref[...])
        ).astype(BF16)

        @pl.when(section == 1)
        def _():
            pass_on(ig_stage, gin, gin_sem, m, 1).start()

        start_emit(ig_stage, ig_ref, 1, m)

    def backward_tick(i, carry):
        @pl.when(i < SEQS)
        def _():
            feed_forward_back(i)

        @pl.when(i >= 2)
        def _():
            finish_back(i - 2)

        @pl.when((i >= 1) & (i <= SEQS))
        def _():
            attention_back(i - 1)

        return carry

    lax.fori_loop(0, SEQS + 2, backward_tick, 0)

    def flush(out, slot, col):
        return pltpu.make_async_copy(
            g_stage.at[slot], out.at[:, pl.ds(col, 128)], g_sem.at[slot]
        )

    def product(left, right, right_col, out, col, count):
        def step(j, carry):
            slot = lax.rem(j, 2)

            @pl.when(j >= 2)
            def _():
                flush(out, slot, 0).wait()

            start = pl.multiple_of(j * 128, 128)
            g_stage[slot] = dot(left[...], right[:, pl.ds(right_col + start, 128)]).astype(BF16)
            flush(out, slot, pl.multiple_of(col + start, 128)).start()
            return carry

        lax.fori_loop(0, count, step, 0)
        flush(out, 0, 0).wait()
        flush(out, 1, 0).wait()

    def features(source):
        xt[...] = dot_nt(place_ref[...], source[...]).astype(BF16)

    features(gin)
    product(xt, hidden, 0, g0_ref, 0, 12)
    features(ffn_in)
    product(xt, gates, 0, g1_ref, 0, 12)
    product(xt, ups, 0, g2_ref, 0, 12)
    features(attn_in)
    product(xt, mixed, 0, g3_ref, 0, 4)
    gains = jnp.concatenate(
        [jnp.zeros((64, WIDTH), F32), gain_acc[...], jnp.zeros((56, WIDTH), F32)], axis=0
    ).astype(BF16)
    g_stage[0] = (dot(xt[...], mixed[:, 512:640]) + dot_nt(place_ref[...], gains)).astype(BF16)
    flush(g3_ref, 0, 512).start()
    flush(g3_ref, 0, 512).wait()
    features(normed)
    product(xt, qkv_back, 0, g3_ref, 640, 8)

    def drain(m, carry):
        for phase in range(4):
            exchange(phase, m).wait_send()
        for s, (source, target, sem) in enumerate(((x_ref, hin, hin_sem), (cot_ref, gin, gin_sem))):
            @pl.when((section == s) & (shard == 1))
            def _():
                fetch(source, target, sem, m)[1]().wait_send()

        @pl.when(section == 0)
        def _():
            pass_on(act_stage, hin, hin_sem, m, 0).wait_send()

        @pl.when(section == 1)
        def _():
            pass_on(ig_stage, gin, gin_sem, m, 1).wait_send()

        for which, (stage, target) in enumerate(((act_stage, act_ref), (ig_stage, ig_ref))):
            local, push = emit(stage, target, which, m)

            @pl.when(shard == 0)
            def _():
                local().wait()

            @pl.when(shard == 1)
            def _():
                push().wait()

        return carry

    lax.fori_loop(0, SEQS, drain, 0)


def reduce_kernel(g0, g1, g2, g3, o0, o1, o2, o3, *scratch):
    outs = (o0, o1, o2, o3)
    rep = lax.axis_index("replica")
    y, z, x = lax.div(rep, 2 * RING), lax.rem(lax.div(rep, RING), 2), lax.rem(rep, RING)

    def device(yy, zz, xx):
        return {"replica": (yy * 2 + zz) * RING + xx}

    def step(v, by):
        return lax.rem(v + by + RING, RING)

    near = {
        "y": (device(step(y, 1), z, x), device(step(y, -1), z, x), y),
        "x": (device(y, z, step(x, 1)), device(y, z, step(x, -1)), x),
    }
    side = device(y, 1 - z, x)

    barrier = pltpu.get_barrier_semaphore()
    for target in (near["y"][0], near["y"][1], near["x"][0], near["x"][1], side):
        pl.semaphore_signal(barrier, inc=1, device_id=target, device_id_type=MESH)
    pl.semaphore_wait(barrier, 5)

    count = len(BLOCKS)
    send, recv, here = scratch[-3:]
    buffers = [scratch[12 * b:12 * (b + 1)] for b in range(count)]
    gs = (g0, g1, g2, g3)

    def remote(b, k, source, target, to):
        return pltpu.make_async_remote_copy(
            source, target, send.at[b, k], recv.at[b, k], device_id=to, device_id_type=MESH
        )

    def make(b):
        part, col, wide, cut = BLOCKS[b]
        axis = PARTS[part][1]
        other = "x" if axis == "y" else "y"
        right, left, me = near[axis]
        right2, left2, me2 = near[other]
        r1a, r1b, r2l, r2r, c1, c2, h, s1a, s1b, t2l, t2r, zz = buffers[b]
        zs, zr = zz.at[0:PIECE], zz.at[PIECE:PIECE + 48]
        fa, fb = pl.ds(0, cut), pl.ds(cut, wide - cut)
        ga, gb, gw = pl.ds(col, cut), pl.ds(col + cut, wide - cut), pl.ds(col, wide)
        g = gs[part]

        def chunk(by, cols):
            t = step(me, by)
            return g.at[t, :, :, cols] if axis == "y" else g.at[:, t, :, cols]

        plus2, minus2 = step(me2, 1), step(me2, -1)
        far2 = step(me2, 2)
        first = [
            remote(b, 0, chunk(2, ga), r1a, right),
            remote(b, 1, chunk(2, gb), r1b, left),
            remote(b, 2, chunk(1, gb), r2l.at[:, :, fb], right),
            remote(b, 3, chunk(-1, ga), r2r.at[:, :, fa], left),
        ]
        locals_ = [
            pltpu.make_async_copy(chunk(1, ga), c1, here.at[b, 0]),
            pltpu.make_async_copy(chunk(-1, gb), c2, here.at[b, 1]),
            pltpu.make_async_copy(chunk(0, gw), h, here.at[b, 2]),
        ]
        second = [
            remote(b, 4, c1, r2l.at[:, :, fa], right),
            remote(b, 5, c2, r2r.at[:, :, fb], left),
        ]
        third = [
            remote(b, 6, h.at[far2, :, fa], s1a, right2),
            remote(b, 7, h.at[far2, :, fb], s1b, left2),
            remote(b, 8, h.at[plus2, :, fb], t2l.at[:, fb], right2),
            remote(b, 9, h.at[minus2, :, fa], t2r.at[:, fa], left2),
        ]
        fourth = [
            remote(b, 10, h.at[plus2, :, fa], t2l.at[:, fa], right2),
            remote(b, 11, h.at[minus2, :, fb], t2r.at[:, fb], left2),
        ]
        fifth = [
            remote(b, 12, zz.at[pl.ds(pl.multiple_of(32 * (1 - z), 16), 48)], zr, side),
        ]

        def run_a():
            for copy in first + locals_:
                copy.start()

        def run_b():
            first[0].wait_recv()
            locals_[0].wait()
            c1[...] = (c1[...].astype(F32) + r1a[...].astype(F32)).astype(BF16)
            second[0].start()
            first[1].wait_recv()
            locals_[1].wait()
            c2[...] = (c2[...].astype(F32) + r1b[...].astype(F32)).astype(BF16)
            second[1].start()

        def run_c():
            for copy in first[2:] + second:
                copy.wait_recv()
            locals_[2].wait()
            h[...] = (
                h[...].astype(F32) + r2l[...].astype(F32) + r2r[...].astype(F32)
            ).astype(BF16)
            for copy in third:
                copy.start()

        def run_d():
            third[0].wait_recv()
            h[plus2, :, 0:cut] = (
                h[plus2, :, 0:cut].astype(F32) + s1a[...].astype(F32)
            ).astype(BF16)
            fourth[0].start()
            third[1].wait_recv()
            h[minus2, :, cut:wide] = (
                h[minus2, :, cut:wide].astype(F32) + s1b[...].astype(F32)
            ).astype(BF16)
            fourth[1].start()

        def run_e():
            for copy in third[2:] + fourth:
                copy.wait_recv()
            zz[0:PIECE] = (
                h[me2].astype(F32) + t2l[...].astype(F32) + t2r[...].astype(F32)
            ).astype(BF16)
            fifth[0].start()

        def run_f():
            fifth[0].wait_recv()
            mine = zz[0:PIECE].astype(F32)
            theirs = zz[PIECE:PIECE + 48].astype(F32)
            low = z == 0
            outs[part][:, col:col + wide] = jnp.where(
                low, mine[0:40] + theirs[0:40], mine[40:80] + theirs[8:48]
            )

        def finish():
            for copy in first + second + third + fourth + fifth:
                copy.wait_send()

        return (run_a, run_f, run_e, run_d, run_c, run_b, finish)

    made = [make(b) for b in range(count)]
    for t in range(count + 5):
        for which, late in ((0, 0), (1, 5), (2, 4), (3, 3), (4, 2), (5, 1)):
            if 0 <= t - late < count:
                made[t - late][which]()
    for b in range(count):
        made[b][6]()


def on_device(x, cot, ga, wq, wk, wv, wo, gf, wg, wu, wd):
    cosine, sine = rope_tables()
    vmem = pl.BlockSpec(memory_space=pltpu.VMEM)
    any_ = pl.BlockSpec(memory_space=pl.ANY)
    sds = jax.ShapeDtypeStruct
    rows = (TOKENS, WIDTH)
    dma = pltpu.SemaphoreType.DMA
    outs = pl.pallas_call(
        compute_kernel,
        out_shape=[sds(x.shape, BF16)] * 2 + [sds((ROWS, part[0]), BF16) for part in PARTS],
        in_specs=[any_] * 2 + [vmem] * 13,
        out_specs=[any_] * 6,
        scratch_shapes=[
            pltpu.VMEM((WIDTH, QW), BF16),
            pltpu.VMEM((WIDTH, KW), BF16),
            pltpu.VMEM(rows, BF16),
            pltpu.VMEM(rows, BF16),
            pltpu.VMEM(rows, BF16),
            pltpu.VMEM((TOKENS, QW), BF16),
            pltpu.VMEM((TOKENS, QW), BF16),
            pltpu.VMEM((TOKENS, KW), BF16),
            pltpu.VMEM((TOKENS, KW), BF16),
            pltpu.VMEM((TOKENS, KW), BF16),
            pltpu.VMEM((SEQS, GROUPS, 3 * LEN, LEN), BF16),
            pltpu.VMEM((TOKENS, 640), BF16),
            pltpu.VMEM(rows, F32),
            pltpu.VMEM(rows, BF16),
            pltpu.VMEM((TOKENS, FF), BF16),
            pltpu.VMEM((TOKENS, FF), BF16),
            pltpu.VMEM((TOKENS, FF), BF16),
            pltpu.VMEM(rows, BF16),
            pltpu.VMEM((TOKENS, 1024), BF16),
            pltpu.VMEM((8, WIDTH), F32),
            pltpu.VMEM((ROWS, TOKENS), BF16),
            pltpu.VMEM((4,) + rows, BF16),
            pltpu.VMEM((4,) + rows, BF16),
            pltpu.VMEM(rows, BF16),
            pltpu.VMEM(rows, BF16),
            pltpu.VMEM((2, ROWS, 128), BF16),
            dma((SEQS,)),
            dma((SEQS,)),
            dma((SEQS,)),
            dma((SEQS,)),
            dma((4, SEQS)),
            dma((4, SEQS)),
            dma((2, SEQS)),
            dma((2, SEQS)),
            dma((2, SEQS)),
            dma((2,)),
        ],
        compiler_params=pltpu.CompilerParams(
            collective_id=0, has_side_effects=True, vmem_limit_bytes=63 * 2**20
        ),
        cost_estimate=pl.CostEstimate(
            flops=26 * 10**9, bytes_accessed=36 * 10**6, transcendentals=10**7
        ),
        name="layer",
    )(
        x, cot, ga, wq[0], wk[0], wv[0], wo[0], gf, wg[0], wu[0], wd[0],
        jnp.asarray(cosine), jnp.asarray(sine),
        jnp.asarray(turn_matrix(), BF16), jnp.asarray(place_matrix(), BF16),
    )
    acts, grads, *gs = outs
    buffers = []
    for part, col, wide, cut in BLOCKS:
        rest = wide - cut
        buffers += [
            pltpu.VMEM((RING, PIECE, cut), BF16),
            pltpu.VMEM((RING, PIECE, rest), BF16),
            pltpu.VMEM((RING, PIECE, wide), BF16),
            pltpu.VMEM((RING, PIECE, wide), BF16),
            pltpu.VMEM((RING, PIECE, cut), BF16),
            pltpu.VMEM((RING, PIECE, rest), BF16),
            pltpu.VMEM((RING, PIECE, wide), BF16),
            pltpu.VMEM((PIECE, cut), BF16),
            pltpu.VMEM((PIECE, rest), BF16),
            pltpu.VMEM((PIECE, wide), BF16),
            pltpu.VMEM((PIECE, wide), BF16),
            pltpu.VMEM((PIECE + 48, wide), BF16),
        ]
    n = len(BLOCKS)
    down, gate, up, mix = pl.pallas_call(
        reduce_kernel,
        out_shape=[sds((40, part[0]), F32) for part in PARTS],
        in_specs=[any_] * 4,
        out_specs=[vmem] * 4,
        scratch_shapes=buffers + [dma((n, 13)), dma((n, 13)), dma((n, 3))],
        compiler_params=pltpu.CompilerParams(
            collective_id=1, has_side_effects=True, vmem_limit_bytes=60 * 2**20
        ),
        name="reduce",
    )(*[g.reshape(RING, RING, PIECE, part[0]) for g, part in zip(gs, PARTS)])
    mix = mix[:OWN]
    return (
        acts[None],
        grads[None],
        mix[:, QW + 1][None],
        mix[:, 640:640 + QW][None],
        mix[:, 640 + QW:640 + QW + KW][None],
        mix[:, 640 + QW + KW:640 + QW + 2 * KW][None],
        mix[:, :QW].T[None],
        mix[:, QW][None],
        gate[:OWN][None],
        up[:OWN][None],
        down[:OWN].T[None],
    )


def solution(mesh):
    in_specs = (
        P("replica", None, None),
        P("replica", None, None),
        P("section", None),
        P("section", None, "shard"),
        P("section", None, "shard"),
        P("section", None, "shard"),
        P("section", "shard", None),
        P("section", None),
        P("section", None, "shard"),
        P("section", None, "shard"),
        P("section", "shard", None),
    )
    out_specs = (
        P("section", "replica", None, None),
        P("section", "replica", None, None),
        P("section", "replica"),
        P("section", "replica", "shard"),
        P("section", "replica", "shard"),
        P("section", "replica", "shard"),
        P("section", "shard", "replica"),
        P("section", "replica"),
        P("section", "replica", "shard"),
        P("section", "replica", "shard"),
        P("section", "shard", "replica"),
    )
    return jax.shard_map(
        on_device, mesh=mesh, in_specs=in_specs, out_specs=out_specs, check_vma=False
    )
```

```python
import jax
import jax.numpy as jnp
import numpy as np
from jax import lax
from jax.experimental import pallas as pl
from jax.experimental.pallas import tpu as pltpu
from jax.sharding import PartitionSpec as P

HEAD = 64
HEADS = 9
GROUPS = 3
WIDTH = 1152
FF = 1536
LEN = 128
SEQS = 4
TOKENS = LEN * SEQS
QW = HEADS * HEAD
KW = GROUPS * HEAD
RING = 4
PIECE = 80
ROWS = RING * RING * PIECE
OWN = WIDTH // 32
EPSILON = 1e-05
ROPE_BASE = 10000.0
F32 = jnp.float32
BF16 = jnp.bfloat16
MESH = pl.DeviceIdType.MESH
PARTS = (1536, 1536, 1536, 1664)
BLOCKS = (
    (0, 0, 768, 384, "x"),
    (0, 768, 768, 384, "y"),
    (1, 0, 768, 384, "x"),
    (1, 768, 768, 384, "y"),
    (2, 0, 768, 384, "x"),
    (2, 768, 768, 384, "y"),
    (3, 0, 640, 384, "y"),
    (3, 640, 512, 256, "x"),
    (3, 1152, 256, 128, "x"),
    (3, 1408, 256, 128, "y"),
)
COUNT = len(BLOCKS)
COLUMNS = sum(PARTS)
WIDE = max(block[2] for block in BLOCKS)
C_SLOTS, L_SLOTS, H_SLOTS, G_SLOTS = 7, 4, 5, 4


def dot(left, right):
    return lax.dot_general(left, right, (((1,), (0,)), ((), ())), preferred_element_type=F32)


def dot_nt(left, right):
    return lax.dot_general(left, right, (((1,), (1,)), ((), ())), preferred_element_type=F32)


def dot_tn(left, right):
    return lax.dot_general(left, right, (((0,), (0,)), ((), ())), preferred_element_type=F32)


def rope_tables():
    half = HEAD // 2
    position = np.arange(LEN, dtype=np.float32)
    frequency = (ROPE_BASE ** (-np.arange(half, dtype=np.float32) * 2.0 / HEAD)).astype(np.float32)
    angles = position[:, None] * frequency[None, :]
    cosine = np.cos(angles).astype(np.float32)
    sine = np.sin(angles).astype(np.float32)
    return (
        np.tile(np.concatenate([cosine, cosine], 1), (1, 2)),
        np.tile(np.concatenate([sine, sine], 1), (1, 2)),
    )


def turn_matrix():
    turn = np.zeros((128, 128), np.float32)
    for head in range(2):
        for j in range(HEAD // 2):
            first, second = head * HEAD + j, head * HEAD + HEAD // 2 + j
            turn[second, first] = -1.0
            turn[first, second] = 1.0
    return turn


def place_matrix():
    place = np.zeros((RING, RING, PIECE, WIDTH), np.float32)
    for y in range(RING):
        for x in range(RING):
            for z in range(2):
                owner = (y * 2 + z) * RING + x
                for i in range(OWN):
                    place[y, x, z * 40 + i, owner * OWN + i] = 1.0
    return place.reshape(ROWS, WIDTH)


def rms_factor(rows):
    return lax.rsqrt(jnp.mean(rows * rows, axis=-1, keepdims=True) + EPSILON)


def norm_back(rows, factor, grad):
    return factor * grad - rows * factor**3 * jnp.mean(grad * rows, axis=-1, keepdims=True)


def rows_of(first, count):
    return pl.ds(pl.multiple_of(first * LEN, LEN), count * LEN)


class Ring:
    def __init__(self, gs, outs, r2l, r2r, r1, cs, hs, ls, rs, second, send, recv, here):
        self.gs, self.outs, self.r2l, self.r2r = gs, outs, r2l, r2r
        self.r1, self.cs, self.hs, self.ls, self.rs = r1, cs, hs, ls, rs
        self.second, self.send, self.recv, self.here = second, send, recv, here
        rep = lax.axis_index("replica")
        y, z, x = lax.div(rep, 2 * RING), lax.rem(lax.div(rep, RING), 2), lax.rem(rep, RING)
        self.z = z

        def device(yy, zz, xx):
            return {"replica": (yy * 2 + zz) * RING + xx}

        self.near = {
            "y": (device(self.turn(y, 1), z, x), device(self.turn(y, -1), z, x), y),
            "x": (device(y, z, self.turn(x, 1)), device(y, z, self.turn(x, -1)), x),
        }
        self.side = device(y, 1 - z, x)
        self.made = [self.make(b) for b in range(COUNT)]
        self.sent = set()
        self.steps = dict(
            a=self.a, b0=self.b0, b=self.b, c0=self.c0, c=self.c, d=self.d, e=self.e, f=self.f
        )

    @staticmethod
    def turn(v, by):
        return lax.rem(v + by + RING, RING)

    def neighbours(self):
        return self.near["y"][:2] + self.near["x"][:2]

    def make(self, b):
        part, col, wide, cut, axis = BLOCKS[b]
        base = sum(block[2] for block in BLOCKS[:b])
        right, left, me = self.near[axis]
        right2, left2, me2 = self.near["x" if axis == "y" else "y"]
        r1a, r1b = self.r1[2 * b:2 * b + 2]
        s1a, s1b, t2l, t2r, zz = self.second[5 * b:5 * b + 5]
        cs, ls, rs, hs = b % C_SLOTS, b % L_SLOTS, b % L_SLOTS, b % H_SLOTS
        c = self.cs.at[cs]
        r2l, r2r = self.r2l, self.r2r
        rest = wide - cut
        g = self.gs[part]

        def remote(k, source, target, to):
            return pltpu.make_async_remote_copy(
                source, target, self.send.at[b, k], self.recv.at[b, k],
                device_id=to, device_id_type=MESH,
            )

        def load(k, source, target):
            return pltpu.make_async_copy(source, target, self.here.at[b, k])

        def chunk(by, first, count):
            t = self.turn(me, by)
            cols = pl.ds(col + first, count)
            return g.at[t, :, :, cols] if axis == "y" else g.at[:, t, :, cols]

        def lanes(ref, first, count):
            return ref.at[:, :, pl.ds(first, count)]

        plus2, minus2, far2 = self.turn(me2, 1), self.turn(me2, -1), self.turn(me2, 2)
        fa, fb = pl.ds(0, cut), pl.ds(cut, rest)
        early = dict(
            first=[
                remote(0, chunk(2, 0, cut), r1a, right),
                remote(1, chunk(2, cut, rest), r1b, left),
                remote(2, chunk(1, cut, rest), lanes(r2l, base + cut, rest), right),
                remote(3, chunk(-1, 0, cut), lanes(r2r, base, cut), left),
            ],
            near=[
                load(0, chunk(1, 0, cut), lanes(c, 0, cut)),
                load(1, chunk(-1, cut, rest), lanes(c, cut, rest)),
            ],
        )
        if self.hs is None:
            return early
        l, r, h = self.ls.at[ls], self.rs.at[rs], self.hs.at[hs]
        return dict(
            early,
            second=[
                remote(4, lanes(c, 0, cut), lanes(r2l, base, cut), right),
                remote(5, lanes(c, cut, rest), lanes(r2r, base + cut, rest), left),
            ],
            back=[
                load(2, chunk(0, 0, wide), lanes(h, 0, wide)),
                load(3, lanes(r2l, base, wide), lanes(l, 0, wide)),
                load(4, lanes(r2r, base, wide), lanes(r, 0, wide)),
            ],
            third=[
                remote(6, h.at[far2, :, fa], s1a, right2),
                remote(7, h.at[far2, :, fb], s1b, left2),
                remote(8, h.at[plus2, :, fb], t2l.at[:, fb], right2),
                remote(9, h.at[minus2, :, fa], t2r.at[:, fa], left2),
            ],
            fourth=[
                remote(10, h.at[plus2, :, fa], t2l.at[:, fa], right2),
                remote(11, h.at[minus2, :, fb], t2r.at[:, fb], left2),
            ],
            fifth=[
                remote(
                    12,
                    zz.at[pl.ds(pl.multiple_of(32 * (1 - self.z), 16), 48)],
                    zz.at[pl.ds(PIECE, 48)],
                    self.side,
                ),
            ],
        )

    def settle(self, b, *names):
        for name in names:
            if (b, name) not in self.sent:
                self.sent.add((b, name))
                for copy in self.made[b][name]:
                    copy.wait_send()

    def a(self, b):
        for copy in self.made[b]["first"]:
            copy.start()

    def b0(self, b):
        if b >= C_SLOTS:
            self.settle(b - C_SLOTS, "second")
        for copy in self.made[b]["near"]:
            copy.start()

    def b(self, b):
        _, _, wide, cut, _ = BLOCKS[b]
        m = self.made[b]
        slot = b % C_SLOTS
        for k, (first, last) in enumerate(((0, cut), (cut, wide))):
            m["first"][k].wait_recv()
            m["near"][k].wait()
            self.cs[slot, :, :, first:last] = (
                self.cs[slot, :, :, first:last] + self.r1[2 * b + k][...]
            )
            m["second"][k].start()

    def c0(self, b):
        if b >= H_SLOTS:
            self.settle(b - H_SLOTS, "third", "fourth")
        m = self.made[b]
        for copy in m["first"][2:] + m["second"]:
            copy.wait_recv()
        for copy in m["back"]:
            copy.start()

    def c(self, b):
        wide = BLOCKS[b][2]
        m = self.made[b]
        for copy in m["back"]:
            copy.wait()
        slot, side = b % H_SLOTS, b % L_SLOTS
        total = self.hs[slot, :, :, 0:wide] + (
            self.ls[side, :, :, 0:wide] + self.rs[side, :, :, 0:wide]
        )
        self.hs[slot, :, :, 0:wide] = total
        for copy in m["third"]:
            copy.start()

    def d(self, b):
        _, _, wide, cut, axis = BLOCKS[b]
        m = self.made[b]
        me2 = self.near["x" if axis == "y" else "y"][2]
        slot = b % H_SLOTS
        for k, (by, first, last) in enumerate(((1, 0, cut), (-1, cut, wide))):
            t = self.turn(me2, by)
            m["third"][k].wait_recv()
            self.hs[slot, t, :, first:last] = (
                self.hs[slot, t, :, first:last] + self.second[5 * b + k][...]
            )
            m["fourth"][k].start()

    def e(self, b):
        _, _, wide, _, axis = BLOCKS[b]
        m = self.made[b]
        me2 = self.near["x" if axis == "y" else "y"][2]
        t2l, t2r, zz = self.second[5 * b + 2:5 * b + 5]
        for copy in m["third"][2:] + m["fourth"]:
            copy.wait_recv()
        total = self.hs[b % H_SLOTS, me2, :, 0:wide] + (t2l[...] + t2r[...])
        zz[0:PIECE] = total
        m["fifth"][0].start()

    def f(self, b):
        part, col, wide, _, _ = BLOCKS[b]
        self.made[b]["fifth"][0].wait_recv()
        zz = self.second[5 * b + 4]
        mine = zz[0:PIECE].astype(F32)
        theirs = zz[PIECE:PIECE + 48].astype(F32)
        self.outs[part][:, col:col + wide] = jnp.where(
            self.z == 0, mine[0:40] + theirs[0:40], mine[40:80] + theirs[8:48]
        )

    def finish(self):
        for b in range(COUNT):
            self.settle(b, "first", "second", "third", "fourth", "fifth")

    def run(self, *words):
        for word in words:
            self.steps[word[:-1]](int(word[-1]))


def layer_kernel(
    x_ref, cot_ref, ga_ref, gf_ref,
    wq_in, wk_in, wv_in, wo_in, cos_in, sin_in, turn_in, wg_in, wu_in, wd_in, place_in,
    act_ref, ig_ref, g0, g1, g2, g3, r2l, r2r, o0, o1, o2, o3,
    *scratch,
):
    (
        wq_ref, wk_ref, wv_ref, wo_ref, cos_ref, sin_ref, turn_ref, wd_ref, place_ref,
        hin, gin, normed, qs, ks, vs, probs, mixed, middle, ffn_in, gates, ups, hidden,
        qkv_back, gain_acc, xt, middle_back, snd_a, rcv_a, snd_b, rcv_b, g_stage, cs,
    ) = scratch[:32]
    r1 = scratch[32:32 + 2 * COUNT]
    stage2 = scratch[32 + 2 * COUNT:32 + 7 * COUNT]
    (
        load_sem, in_sem, in_send, ar_send, ar_recv, step_send, step_recv, out_sem, out_send, g_sem,
        ring_send, ring_recv, ring_here,
    ) = scratch[32 + 7 * COUNT:]
    section = lax.axis_index("section")
    shard = lax.axis_index("shard")
    rep = lax.axis_index("replica")
    zlo = lax.rem(lax.div(rep, RING), 2)
    side = rep + RING - 2 * RING * zlo
    core = {"section": 1 - section}
    twin = {"shard": 1 - shard, "replica": side}
    swap = {"replica": side}

    def make_ring(hs, ls, rs):
        return Ring(
            (g0, g1, g2, g3), (o0, o1, o2, o3), r2l, r2r, r1, cs, hs, ls, rs, stage2,
            ring_send, ring_recv, ring_here,
        )

    ring = make_ring(None, None, None)
    wide_weights = []

    loads = [
        pltpu.make_async_copy(source, target, load_sem.at[k])
        for k, (source, target) in enumerate(
            (
                (wq_in, wq_ref), (wk_in, wk_ref), (wv_in, wv_ref), (cos_in, cos_ref),
                (sin_in, sin_ref), (turn_in, turn_ref), (wo_in, wo_ref), (wd_in, wd_ref),
                (place_in, place_ref),
            )
        )
    ]
    for copy in loads[:7]:
        copy.start()

    barrier = pltpu.get_barrier_semaphore()
    near = (core, twin, swap) + ring.neighbours()
    for target in near:
        pl.semaphore_signal(barrier, inc=1, device_id=target, device_id_type=MESH)
    pl.semaphore_wait(barrier, len(near))

    inputs = ((x_ref, hin), (cot_ref, gin))

    def fetch(s, m):
        source, target = inputs[s]
        rows = rows_of(m, 1)

        def local():
            return pltpu.make_async_copy(source.at[m], target.at[rows], in_sem.at[s, m])

        def push():
            return pltpu.make_async_remote_copy(
                source.at[m], target.at[rows], in_send.at[s, m], in_sem.at[s, m],
                device_id=swap, device_id_type=MESH,
            )

        return local, push

    for m in range(SEQS):
        for s in range(2):
            local, push = fetch(s, m)

            @pl.when((section == s) & (shard == 0))
            def _():
                local().start()

            @pl.when((section == s) & (shard == 1))
            def _():
                push().start()

    for copy in loads[7:]:
        copy.start()

    def wait_input(s, m):
        local, push = fetch(s, m)

        @pl.when(shard == 0)
        def _():
            local().wait()

        @pl.when(shard == 1)
        def _():
            push().wait_recv()

    def pass_on(which, first, count, k):
        source, target = ((snd_b, hin), (snd_a, gin))[which]
        rows = rows_of(first, count)
        return pltpu.make_async_remote_copy(
            source.at[rows], target.at[rows], step_send.at[which, k], step_recv.at[which, k],
            device_id=core, device_id_type=MESH,
        )

    halves = ((snd_a, rcv_a), (snd_b, rcv_b), (snd_b, rcv_b), (snd_a, rcv_a))

    def exchange(phase, first, count, k):
        snd, rcv = halves[phase]
        rows = rows_of(first, count)
        return pltpu.make_async_remote_copy(
            snd.at[rows], rcv.at[rows], ar_send.at[phase, k], ar_recv.at[phase, k],
            device_id=twin, device_id_type=MESH,
        )

    def offer(phase, first, count, k, value):
        halves[phase][0][rows_of(first, count), :] = value.astype(BF16)
        exchange(phase, first, count, k).start()

    def exchanged(phase, first, count, k):
        exchange(phase, first, count, k).wait()
        snd, rcv = halves[phase]
        rows = rows_of(first, count)
        return snd[rows, :].astype(F32) + rcv[rows, :].astype(F32)

    def emit(which, m):
        source, target = ((snd_b, act_ref), (snd_a, ig_ref))[which]
        rows = rows_of(m, 1)

        def local():
            return pltpu.make_async_copy(source.at[rows], target.at[m], out_sem.at[which, m])

        def push():
            return pltpu.make_async_remote_copy(
                source.at[rows], target.at[m], out_send.at[which, m], out_sem.at[which, m],
                device_id=swap, device_id_type=MESH,
            )

        return local, push

    def start_emit(which, m):
        local, push = emit(which, m)

        @pl.when(shard == 0)
        def _():
            local().start()

        @pl.when(shard == 1)
        def _():
            push().start()

    def settle_emit(which, m):
        local, push = emit(which, m)

        @pl.when(shard == 0)
        def _():
            local().wait()

        @pl.when(shard == 1)
        def _():
            push().wait_send()

    gain_acc[...] = jnp.zeros_like(gain_acc)
    mixed[:, QW:] = jnp.zeros((TOKENS, 64), BF16)
    qkv_back[:, QW + 2 * KW:] = jnp.zeros((TOKENS, 64), BF16)

    def stacked(value, g):
        return jnp.concatenate(
            [value[:, (3 * g + j) * HEAD:(3 * g + j + 1) * HEAD] for j in range(3)], axis=0
        )

    def turned(value):
        wide = value.shape[1]
        return jnp.concatenate(
            [
                dot(value[:, c:min(c + 128, wide)], turn_ref[:min(128, wide - c), :min(128, wide - c)])
                for c in range(0, wide, 128)
            ],
            axis=1,
        )

    def spread(table, wide):
        return jnp.concatenate(
            [table[:, :min(128, wide - c)] for c in range(0, wide, 128)], axis=1
        )

    def rope(value):
        high = value.astype(BF16)
        low = (value - high.astype(F32)).astype(BF16)
        wide = value.shape[1]
        cosine, sine = spread(cos_ref[...], wide), spread(sin_ref[...], wide)
        return (value * cosine + (turned(high) + turned(low)) * sine).astype(BF16)

    def attention(m):
        rows = rows_of(m, 1)

        @pl.when(section == 0)
        def _():
            wait_input(0, m)

        @pl.when(section == 1)
        def _():
            pass_on(0, m, 1, m).wait_recv()

        h = hin[rows, :].astype(F32)
        normal = (h * rms_factor(h) * ga_ref[...]).astype(BF16)
        normed[rows, :] = normal
        query = rope(dot_nt(normal, wq_ref[...]))
        key = rope(dot_nt(normal, wk_ref[...]))
        value = dot_nt(normal, wv_ref[...]).astype(BF16)
        qs[rows, :] = query
        ks[rows, :] = key
        vs[rows, :] = value
        at = lax.rem(lax.broadcasted_iota(jnp.int32, (3 * LEN, LEN), 0), LEN)
        causal = at >= lax.broadcasted_iota(jnp.int32, (3 * LEN, LEN), 1)
        heads = []
        for g in range(GROUPS):
            cols = slice(g * HEAD, (g + 1) * HEAD)
            scores = dot_nt(stacked(query, g), key[:, cols]) * HEAD**-0.5
            scores = jnp.where(causal, scores, -1e30)
            top = jnp.max(scores, axis=-1, keepdims=True)
            weight = jnp.exp(scores - top)
            prob = (weight / jnp.sum(weight, axis=-1, keepdims=True)).astype(BF16)
            probs[m, g] = prob
            out = dot(prob, value[:, cols]).astype(BF16)
            heads += [out[j * LEN:(j + 1) * LEN] for j in range(3)]
        mix = jnp.concatenate(heads, axis=1)
        mixed[rows, :QW] = mix
        offer(0, m, 1, m, dot(mix, wo_ref[...]))

    def feed_forward(m):
        rows = rows_of(m, 1)
        mid = hin[rows, :].astype(F32) + exchanged(0, m, 1, m)
        middle[rows, :] = mid
        normal = (mid * rms_factor(mid) * gf_ref[...]).astype(BF16)
        ffn_in[rows, :] = normal
        for j in range(0, FF, 512):
            cols = slice(j, j + 512)
            gate = dot(normal, wide_weights[0][:, cols])
            up = dot(normal, wide_weights[1][:, cols])
            gates[rows, cols] = gate.astype(BF16)
            ups[rows, cols] = up.astype(BF16)
            hidden[rows, cols] = (gate * jax.nn.sigmoid(gate) * up).astype(BF16)

        @pl.when(section == 0)
        def _():
            offer(1, m, 1, m, dot(hidden[rows, :], wd_ref[...]))

    def finish(first, count, k):
        value = exchanged(1, first, count, k)
        rows = rows_of(first, count)
        snd_b[rows, :] = (middle[rows, :] + value).astype(BF16)

    def feed_forward_back(j):
        rows = rows_of(2 * j, 2)

        @pl.when(section == 1)
        def _():
            wait_input(1, 2 * j)
            wait_input(1, 2 * j + 1)

        @pl.when(section == 0)
        def _():
            for m in (2 * j, 2 * j + 1):
                pass_on(1, m, 1, m).wait_recv()

        down_in = gin[rows, :]
        total = jnp.zeros((2 * LEN, WIDTH), F32)
        for c in range(0, FF, 512):
            cols = slice(c, c + 512)
            back = dot_nt(down_in, wd_ref[cols, :])
            gate = gates[rows, cols].astype(F32)
            up = ups[rows, cols].astype(F32)
            sig = jax.nn.sigmoid(gate)
            gate_back = (back * up * sig * (1.0 + gate * (1.0 - sig))).astype(BF16)
            up_back = (back * gate * sig).astype(BF16)
            gates[rows, cols] = gate_back
            ups[rows, cols] = up_back
            total += dot_nt(gate_back, wide_weights[0][:, cols]) + dot_nt(up_back, wide_weights[1][:, cols])
        for i in range(2):
            offer(2, 2 * j + i, 1, 2 * j + i, total[i * LEN:(i + 1) * LEN])

    def attention_back(m):
        rows = rows_of(m, 1)
        back = exchanged(2, m, 1, m)
        mid = middle[rows, :]
        factor = rms_factor(mid)
        gain_acc[0:1, :] += jnp.sum(back * mid * factor, axis=0, keepdims=True)
        mid_back = gin[rows, :].astype(F32) + norm_back(mid, factor, back * gf_ref[...])
        middle_back[rows, :] = mid_back
        mixed_back = dot_nt(mid_back.astype(BF16), wo_ref[...]).astype(BF16)
        cosine, sine = cos_ref[:, :HEAD], sin_ref[:, :HEAD]
        query, key, value = qs[rows, :], ks[rows, :], vs[rows, :]
        query_turn = turned(query).astype(BF16)
        key_turn = turned(key).astype(BF16)
        query_out, key_out, value_out = [], [], []
        for g in range(GROUPS):
            cols = slice(g * HEAD, (g + 1) * HEAD)
            prob = probs[m, g]
            prob_f = prob.astype(F32)
            out_back = stacked(mixed_back, g)
            value_out.append(dot_tn(prob, out_back).astype(BF16))
            prob_back = dot_nt(out_back, value[:, cols])
            score_back = (
                prob_f * (prob_back - jnp.sum(prob_back * prob_f, axis=-1, keepdims=True))
            ).astype(BF16)
            both = jnp.concatenate([key[:, cols], key_turn[:, cols]], axis=1)
            both_back = dot(score_back, both) * HEAD**-0.5
            for t in range(3):
                one = both_back[t * LEN:(t + 1) * LEN]
                query_out.append((one[:, :HEAD] * cosine - one[:, HEAD:] * sine).astype(BF16))
            both = jnp.concatenate([stacked(query, g), stacked(query_turn, g)], axis=1)
            one = dot_tn(score_back, both) * HEAD**-0.5
            key_out.append((one[:, :HEAD] * cosine - one[:, HEAD:] * sine).astype(BF16))
        qkv_back[rows, :QW + 2 * KW] = jnp.concatenate(query_out + key_out + value_out, axis=1)
        offer(
            3, m, 1, m,
            dot(qkv_back[rows, :QW], wq_ref[...])
            + dot(qkv_back[rows, QW:QW + KW], wk_ref[...])
            + dot(qkv_back[rows, QW + KW:QW + 2 * KW], wv_ref[...]),
        )

    def finish_back(m):
        rows = rows_of(m, 1)
        back = exchanged(3, m, 1, m)
        h = hin[rows, :].astype(F32)
        factor = rms_factor(h)
        gain_acc[1:2, :] += jnp.sum(back * h * factor, axis=0, keepdims=True)
        snd_a[rows, :] = (
            middle_back[rows, :] + norm_back(h, factor, back * ga_ref[...])
        ).astype(BF16)

        @pl.when(section == 1)
        def _():
            pass_on(1, m, 1, m).start()

        start_emit(1, m)

    def flush(out, slot, half, col, wide):
        return pltpu.make_async_copy(
            g_stage.at[slot, :, :, :, pl.ds(0, wide)],
            out.at[pl.ds(2 * half, 2), :, :, pl.ds(col, wide)],
            g_sem.at[slot],
        )

    def product(right, right_col, out, col, count):
        def step(k, carry):
            slot, half = lax.rem(k, G_SLOTS), lax.rem(k, 2)

            @pl.when(k >= G_SLOTS)
            def _():
                flush(out, slot, half, 0, 512).wait()

            start = pl.multiple_of(lax.div(k, 2) * 512, 512)
            left = xt[pl.ds(pl.multiple_of(half * 640, 640), 640), :]
            g_stage[slot] = (
                dot(left, right[:, pl.ds(right_col + start, 512)])
                .astype(BF16)
                .reshape(2, RING, PIECE, 512)
            )
            flush(out, slot, half, pl.multiple_of(col + start, 128), 512).start()
            return carry

        lax.fori_loop(0, 2 * count, step, 0)
        for k in range(max(0, 2 * count - G_SLOTS), 2 * count):
            flush(out, k % G_SLOTS, k % 2, 0, 512).wait()

    def features(source):
        for c in range(0, TOKENS, 256):
            block = slice(c, c + 256)
            xt[:, block] = dot_nt(place_ref[...], source[block, :].astype(BF16)).astype(BF16)

    def down_gradient(_):
        features(gin)
        product(hidden, 0, g0, 0, 3)
        ring.run("a0", "a1")

    def gate_gradient(_):
        features(ffn_in)
        product(gates, 0, g1, 0, 3)
        ring.run("a2", "a3", "b00", "b01")
        product(ups, 0, g2, 0, 3)
        ring.run("a4", "a5")

    def out_gradient():
        features(middle_back)
        product(mixed, 0, g3, 0, 1)
        gains = jnp.concatenate(
            [jnp.zeros((64, WIDTH), F32), gain_acc[...], jnp.zeros((56, WIDTH), F32)], axis=0
        ).astype(BF16)
        last = (dot(xt[...], mixed[:, 512:640]) + dot_nt(place_ref[...], gains)).astype(BF16)
        for half in range(2):
            g_stage[half, :, :, :, 0:128] = last[half * 640:half * 640 + 640].reshape(
                2, RING, PIECE, 128
            )
            flush(g3, half, half, 512, 128).start()
        for half in range(2):
            flush(g3, half, half, 512, 128).wait()

    def plan(t, ours, theirs):
        index = jnp.int32(-1)
        for k, (one, other) in enumerate(zip(ours, theirs)):
            if one >= 0 or other >= 0:
                index = jnp.where(t == k, jnp.where(section == 0, one, other), index)
        return index

    def tick(t, carry):
        def do(work, ours, theirs):
            index = plan(t, ours, theirs)

            @pl.when(index >= 0)
            def _():
                work(index)

        def finish_forward(m):
            finish(m, 1, m)
            pass_on(0, m, 1, m).start()
            start_emit(0, m)

        @pl.when(t == 1)
        def _():
            for copy in loads[7:] + wide_loads:
                copy.wait()

        do(
            attention,
            (0, 1, 2, -1, 3, -1, -1, -1, -1, -1, -1, -1, -1, -1),
            (0, 1, 2, -1, -1, 3, -1, -1, -1, -1, -1, -1, -1, -1),
        )
        do(
            finish_forward,
            (-1, -1, -1, -1, 0, 1, 2, 3, -1, -1, -1, -1, -1, -1),
            (-1, -1, -1, -1, -1, -1, -1, -1, -1, -1, -1, -1, -1, -1),
        )
        do(
            feed_forward,
            (-1, -1, 0, 1, 2, 3, -1, -1, -1, -1, -1, -1, -1, -1),
            (-1, -1, 0, 1, 2, -1, -1, 3, -1, -1, -1, -1, -1, -1),
        )

        @pl.when((t == 7) & (section == 0))
        def _():
            for m in range(SEQS):
                pass_on(0, m, 1, m).wait_send()
                settle_emit(0, m)

        do(
            finish_back,
            (-1, -1, -1, -1, -1, -1, -1, -1, -1, -1, -1, 0, 1, 2),
            (-1, -1, -1, -1, -1, -1, -1, 0, 1, -1, -1, 2, 3, -1),
        )
        do(
            feed_forward_back,
            (-1, -1, -1, -1, -1, -1, -1, 0, -1, 1, -1, -1, -1, -1),
            (-1, -1, -1, 0, -1, -1, -1, 1, -1, -1, -1, -1, -1, -1),
        )
        do(
            down_gradient,
            (-1, -1, -1, -1, -1, -1, -1, -1, -1, 0, -1, -1, -1, -1),
            (-1, -1, -1, -1, -1, -1, -1, -1, 0, -1, -1, -1, -1, -1),
        )
        do(
            gate_gradient,
            (-1, -1, -1, -1, -1, -1, -1, -1, -1, 0, -1, -1, -1, -1),
            (-1, -1, -1, -1, -1, -1, -1, -1, -1, -1, 0, -1, -1, -1),
        )
        do(
            attention_back,
            (-1, -1, -1, -1, -1, -1, -1, 0, 1, 2, 3, -1, -1, -1),
            (-1, -1, -1, -1, -1, 0, 1, -1, 2, 3, -1, -1, -1, -1),
        )
        return carry

    wide_loads = []

    def first_phase(wg_ref, wu_ref):
        wide_weights[:] = [wg_ref, wu_ref]
        wide_loads[:] = [
            pltpu.make_async_copy(wg_in, wg_ref, load_sem.at[9]),
            pltpu.make_async_copy(wu_in, wu_ref, load_sem.at[10]),
        ]
        for copy in wide_loads:
            copy.start()
        for copy in loads[:7]:
            copy.wait()
        lax.fori_loop(0, 14, tick, 0)

    pl.run_scoped(first_phase, pltpu.VMEM((WIDTH, FF), BF16), pltpu.VMEM((WIDTH, FF), BF16))

    def second_phase(hs, ls, rs):
        steps = make_ring(hs, ls, rs)
        steps.run("b0", "b1")

        @pl.when(section == 0)
        def _():
            finish_back(3)

        @pl.when(section == 1)
        def _():
            for j in range(2):
                offer(1, 2 * j, 2, j, dot(hidden[rows_of(2 * j, 2), :], wd_ref[...]))

        steps.run("b02", "b03")
        out_gradient()
        steps.run("a6", "b2", "b3", "b04", "b05")
        features(normed)
        product(qkv_back, 0, g3, 640, 1)
        steps.run("a7")
        product(qkv_back, 512, g3, 1152, 1)
        steps.run(
            "a8", "a9", "c00", "c01", "c02", "c03", "b4", "b5", "b06", "b07", "b08", "b09",
            "c0", "c1", "c2", "c3", "b6", "b7", "b8", "b9", "d0", "d1", "c04", "c4",
            "d2", "d3", "e0", "e1", "c05", "c06", "c5", "c6", "e2", "e3", "f0", "f1",
        )

        @pl.when(section == 1)
        def _():
            for j in range(2):
                finish(2 * j, 2, j)
                start_emit(0, 2 * j)
                start_emit(0, 2 * j + 1)

        steps.run(
            "c07", "c08", "c7", "c8", "d4", "d5", "e4", "c09", "d6", "e5", "c9", "d7",
            "d8", "f2", "f3", "d9", "e6", "e7", "e8", "e9", "f4", "f5", "f6", "f7",
            "f8", "f9",
        )
        steps.finish()

    pl.run_scoped(
        second_phase,
        *[
            pltpu.VMEM((slots, RING, PIECE, WIDE), BF16)
            for slots in (H_SLOTS, L_SLOTS, L_SLOTS)
        ],
    )

    for m in range(SEQS):
        for s in range(2):
            @pl.when((section == s) & (shard == 1))
            def _():
                fetch(s, m)[1]().wait_send()

        @pl.when(section == 1)
        def _():
            settle_emit(0, m)

        settle_emit(1, m)

        @pl.when(shard == 1)
        def _():
            for which in range(2):
                emit(which, m)[1]().wait_recv()

    for j in range(SEQS):
        @pl.when(section == 1)
        def _():
            pass_on(1, j, 1, j).wait_send()


def deliver_kernel(
    act_in, ig_in, down, gate, up, mix,
    act, ig, gain_a, query, key, value, out, gain_f, gate_out, up_out, down_out,
):
    act[...] = act_in[...]
    ig[...] = ig_in[...]
    for target, source, first, wide in (
        (query, mix, 640, QW),
        (key, mix, 640 + QW, KW),
        (value, mix, 640 + QW + KW, KW),
        (out, mix, 0, QW),
        (gate_out, gate, 0, FF),
        (up_out, up, 0, FF),
        (down_out, down, 0, FF),
    ):
        target[...] = source[0:OWN, first:first + wide].reshape(OWN, 1, wide)
    gains = mix[:, 512:640].T
    gain_f[...] = gains[64:65, 0:OWN]
    gain_a[...] = gains[65:66, 0:OWN]


def on_device(x, cot, ga, wq, wk, wv, wo, gf, wg, wu, wd):
    cosine, sine = rope_tables()
    vmem = pl.BlockSpec(memory_space=pltpu.VMEM)
    any_ = pl.BlockSpec(memory_space=pl.ANY)
    sds = jax.ShapeDtypeStruct
    rows = (TOKENS, WIDTH)
    dma = pltpu.SemaphoreType.DMA
    operands = (
        wq[0].T, wk[0].T, wv[0].T, wo[0], jnp.asarray(cosine), jnp.asarray(sine),
        jnp.asarray(turn_matrix(), BF16), wg[0], wu[0], wd[0], jnp.asarray(place_matrix(), BF16),
    )

    def buffer(shape, kind=BF16):
        return pltpu.VMEM(shape, kind)

    scratch = [
        buffer(item.shape, item.dtype) for k, item in enumerate(operands) if k not in (7, 8)
    ]
    scratch += [buffer(rows)] * 3
    scratch += [
        buffer((TOKENS, QW)),
        buffer((TOKENS, KW)),
        buffer((TOKENS, KW)),
        buffer((SEQS, GROUPS, 3 * LEN, LEN)),
        buffer((TOKENS, 640)),
        buffer(rows, F32),
        buffer(rows),
        buffer((TOKENS, FF)),
        buffer((TOKENS, FF)),
        buffer((TOKENS, FF)),
        buffer((TOKENS, 1024)),
        buffer((8, WIDTH), F32),
        buffer((ROWS, TOKENS)),
        buffer(rows, F32),
    ]
    scratch += [buffer(rows)] * 4
    scratch += [
        buffer((G_SLOTS, 2, RING, PIECE, 512)),
        buffer((C_SLOTS, RING, PIECE, WIDE)),
    ]
    for _, _, wide, cut, _ in BLOCKS:
        scratch += [buffer((RING, PIECE, cut)), buffer((RING, PIECE, wide - cut))]
    for _, _, wide, cut, _ in BLOCKS:
        scratch += [
            buffer((PIECE, cut)),
            buffer((PIECE, wide - cut)),
            buffer((PIECE, wide)),
            buffer((PIECE, wide)),
            buffer((PIECE + 48, wide)),
        ]
    scratch += [
        dma((len(operands),)),
        dma((2, SEQS)),
        dma((2, SEQS)),
        dma((4, SEQS)),
        dma((4, SEQS)),
        dma((2, SEQS)),
        dma((2, SEQS)),
        dma((2, SEQS)),
        dma((2, SEQS)),
        dma((G_SLOTS,)),
        dma((COUNT, 13)),
        dma((COUNT, 13)),
        dma((COUNT, 5)),
    ]
    outs = pl.pallas_call(
        layer_kernel,
        out_shape=(
            [sds(x.shape, BF16)] * 2
            + [sds((RING, RING, PIECE, columns), BF16) for columns in PARTS]
            + [sds((RING, PIECE, COLUMNS), BF16)] * 2
            + [sds((40, columns), F32) for columns in PARTS]
        ),
        in_specs=[any_] * 2 + [vmem] * 2 + [any_] * len(operands),
        out_specs=[any_] * 8 + [vmem] * 4,
        scratch_shapes=scratch,
        compiler_params=pltpu.CompilerParams(
            collective_id=0, has_side_effects=True, vmem_limit_bytes=63 * 2**20
        ),
        cost_estimate=pl.CostEstimate(
            flops=26 * 10**9, bytes_accessed=60 * 10**6, transcendentals=10**7
        ),
        name="layer",
    )(x, cot, ga, gf, *operands)
    acts, grads = outs[:2]
    done = pl.pallas_call(
        deliver_kernel,
        out_shape=(
            [sds(x.shape, BF16)] * 2
            + [sds((1, OWN), F32)]
            + [sds((OWN, 1, wide), F32) for wide in (QW, KW, KW, QW)]
            + [sds((1, OWN), F32)]
            + [sds((OWN, 1, FF), F32)] * 3
        ),
        in_specs=[vmem] * 6,
        out_specs=[vmem] * 11,
        name="deliver",
    )(acts, grads, *outs[8:])
    act, ig, gain_a, query, key, value, out, gain_f, gate, up, down = done

    def rows_out(item):
        return item.transpose(1, 0, 2)

    def columns_out(item):
        return item.transpose(1, 2, 0)

    return (
        act[None], ig[None], gain_a, rows_out(query), rows_out(key), rows_out(value),
        columns_out(out), gain_f, rows_out(gate), rows_out(up), columns_out(down),
    )


def solution(mesh):
    in_specs = (
        P("replica", None, None),
        P("replica", None, None),
        P("section", None),
        P("section", None, "shard"),
        P("section", None, "shard"),
        P("section", None, "shard"),
        P("section", "shard", None),
        P("section", None),
        P("section", None, "shard"),
        P("section", None, "shard"),
        P("section", "shard", None),
    )
    out_specs = (
        P("section", "replica", None, None),
        P("section", "replica", None, None),
        P("section", "replica"),
        P("section", "replica", "shard"),
        P("section", "replica", "shard"),
        P("section", "replica", "shard"),
        P("section", "shard", "replica"),
        P("section", "replica"),
        P("section", "replica", "shard"),
        P("section", "replica", "shard"),
        P("section", "shard", "replica"),
    )
    return jax.shard_map(
        on_device, mesh=mesh, in_specs=in_specs, out_specs=out_specs, check_vma=False
    )
```

```python
import jax
import jax.numpy as jnp
import numpy as np
from jax import lax
from jax.experimental import pallas as pl
from jax.experimental.pallas import tpu as pltpu
from jax.sharding import PartitionSpec as P

HEAD = 64
HEADS = 9
GROUPS = 3
WIDTH = 1152
FF = 1536
LEN = 128
SEQS = 4
TOKENS = LEN * SEQS
QW = HEADS * HEAD
KW = GROUPS * HEAD
RING = 4
PIECE = 80
ROWS = RING * RING * PIECE
OWN = WIDTH // 32
EPSILON = 1e-05
ROPE_BASE = 10000.0
F32 = jnp.float32
BF16 = jnp.bfloat16
MESH = pl.DeviceIdType.MESH
PARTS = (1536, 1536, 1536, 1664)
BLOCKS = (
    (0, 0, 768, 384, "x"),
    (0, 768, 768, 384, "y"),
    (1, 0, 768, 384, "x"),
    (1, 768, 768, 384, "y"),
    (2, 0, 768, 384, "x"),
    (2, 768, 768, 384, "y"),
    (3, 0, 640, 384, "y"),
    (3, 640, 512, 256, "x"),
    (3, 1152, 256, 128, "x"),
    (3, 1408, 256, 128, "y"),
)
COUNT = len(BLOCKS)
COLUMNS = sum(PARTS)
WIDE = max(block[2] for block in BLOCKS)
C_SLOTS, L_SLOTS, H_SLOTS, G_SLOTS = 7, 4, 5, 4


def dot(left, right):
    return lax.dot_general(left, right, (((1,), (0,)), ((), ())), preferred_element_type=F32)


def dot_nt(left, right):
    return lax.dot_general(left, right, (((1,), (1,)), ((), ())), preferred_element_type=F32)


def dot_tn(left, right):
    return lax.dot_general(left, right, (((0,), (0,)), ((), ())), preferred_element_type=F32)


def rope_tables():
    half = HEAD // 2
    position = np.arange(LEN, dtype=np.float32)
    frequency = (ROPE_BASE ** (-np.arange(half, dtype=np.float32) * 2.0 / HEAD)).astype(np.float32)
    angles = position[:, None] * frequency[None, :]
    cosine = np.cos(angles).astype(np.float32)
    sine = np.sin(angles).astype(np.float32)
    return (
        np.tile(np.concatenate([cosine, cosine], 1), (1, 2)),
        np.tile(np.concatenate([sine, sine], 1), (1, 2)),
    )


def turn_matrix():
    turn = np.zeros((128, 128), np.float32)
    for head in range(2):
        for j in range(HEAD // 2):
            first, second = head * HEAD + j, head * HEAD + HEAD // 2 + j
            turn[second, first] = -1.0
            turn[first, second] = 1.0
    return turn


def place_matrix():
    place = np.zeros((RING, RING, PIECE, WIDTH), np.float32)
    for y in range(RING):
        for x in range(RING):
            for z in range(2):
                owner = (y * 2 + z) * RING + x
                for i in range(OWN):
                    place[y, x, z * 40 + i, owner * OWN + i] = 1.0
    return place.reshape(ROWS, WIDTH)


def rms_factor(rows):
    return lax.rsqrt(jnp.mean(rows * rows, axis=-1, keepdims=True) + EPSILON)


def norm_back(rows, factor, grad):
    return factor * grad - rows * factor**3 * jnp.mean(grad * rows, axis=-1, keepdims=True)


def rows_of(first, count):
    return pl.ds(pl.multiple_of(first * LEN, LEN), count * LEN)


class Ring:
    def __init__(self, gs, outs, r2l, r2r, r1, cs, hs, ls, rs, second, send, recv, here):
        self.gs, self.outs, self.r2l, self.r2r = gs, outs, r2l, r2r
        self.r1, self.cs, self.hs, self.ls, self.rs = r1, cs, hs, ls, rs
        self.second, self.send, self.recv, self.here = second, send, recv, here
        rep = lax.axis_index("replica")
        y, z, x = lax.div(rep, 2 * RING), lax.rem(lax.div(rep, RING), 2), lax.rem(rep, RING)
        self.z = z

        def device(yy, zz, xx):
            return {"replica": (yy * 2 + zz) * RING + xx}

        self.near = {
            "y": (device(self.turn(y, 1), z, x), device(self.turn(y, -1), z, x), y),
            "x": (device(y, z, self.turn(x, 1)), device(y, z, self.turn(x, -1)), x),
        }
        self.side = device(y, 1 - z, x)
        self.made = [self.make(b) for b in range(COUNT)]
        self.sent = set()
        self.steps = dict(
            a=self.a, b0=self.b0, b=self.b, c0=self.c0, c=self.c, d=self.d, e=self.e, f=self.f
        )

    @staticmethod
    def turn(v, by):
        return lax.rem(v + by + RING, RING)

    def neighbours(self):
        return self.near["y"][:2] + self.near["x"][:2]

    def make(self, b):
        part, col, wide, cut, axis = BLOCKS[b]
        base = sum(block[2] for block in BLOCKS[:b])
        right, left, me = self.near[axis]
        right2, left2, me2 = self.near["x" if axis == "y" else "y"]
        r1a, r1b = self.r1[2 * b:2 * b + 2]
        s1a, s1b, t2l, t2r, zz = self.second[5 * b:5 * b + 5]
        cs, ls, rs, hs = b % C_SLOTS, b % L_SLOTS, b % L_SLOTS, b % H_SLOTS
        c = self.cs.at[cs]
        r2l, r2r = self.r2l, self.r2r
        rest = wide - cut
        g = self.gs[part]

        def remote(k, source, target, to):
            return pltpu.make_async_remote_copy(
                source, target, self.send.at[b, k], self.recv.at[b, k],
                device_id=to, device_id_type=MESH,
            )

        def load(k, source, target):
            return pltpu.make_async_copy(source, target, self.here.at[b, k])

        def chunk(by, first, count):
            t = self.turn(me, by)
            cols = pl.ds(col + first, count)
            return g.at[t, :, :, cols] if axis == "y" else g.at[:, t, :, cols]

        def lanes(ref, first, count):
            return ref.at[:, :, pl.ds(first, count)]

        plus2, minus2, far2 = self.turn(me2, 1), self.turn(me2, -1), self.turn(me2, 2)
        fa, fb = pl.ds(0, cut), pl.ds(cut, rest)
        early = dict(
            first=[
                remote(0, chunk(2, 0, cut), r1a, right),
                remote(1, chunk(2, cut, rest), r1b, left),
                remote(2, chunk(1, cut, rest), lanes(r2l, base + cut, rest), right),
                remote(3, chunk(-1, 0, cut), lanes(r2r, base, cut), left),
            ],
            near=[
                load(0, chunk(1, 0, cut), lanes(c, 0, cut)),
                load(1, chunk(-1, cut, rest), lanes(c, cut, rest)),
            ],
        )
        if self.hs is None:
            return early
        l, r, h = self.ls.at[ls], self.rs.at[rs], self.hs.at[hs]
        return dict(
            early,
            second=[
                remote(4, lanes(c, 0, cut), lanes(r2l, base, cut), right),
                remote(5, lanes(c, cut, rest), lanes(r2r, base + cut, rest), left),
            ],
            back=[
                load(2, chunk(0, 0, wide), lanes(h, 0, wide)),
                load(3, lanes(r2l, base, wide), lanes(l, 0, wide)),
                load(4, lanes(r2r, base, wide), lanes(r, 0, wide)),
            ],
            third=[
                remote(6, h.at[far2, :, fa], s1a, right2),
                remote(7, h.at[far2, :, fb], s1b, left2),
                remote(8, h.at[plus2, :, fb], t2l.at[:, fb], right2),
                remote(9, h.at[minus2, :, fa], t2r.at[:, fa], left2),
            ],
            fourth=[
                remote(10, h.at[plus2, :, fa], t2l.at[:, fa], right2),
                remote(11, h.at[minus2, :, fb], t2r.at[:, fb], left2),
            ],
            fifth=[
                remote(
                    12,
                    zz.at[pl.ds(pl.multiple_of(32 * (1 - self.z), 16), 48)],
                    zz.at[pl.ds(PIECE, 48)],
                    self.side,
                ),
            ],
        )

    def settle(self, b, *names):
        for name in names:
            if (b, name) not in self.sent:
                self.sent.add((b, name))
                for copy in self.made[b][name]:
                    copy.wait_send()

    def a(self, b):
        for copy in self.made[b]["first"]:
            copy.start()

    def b0(self, b):
        if b >= C_SLOTS:
            self.settle(b - C_SLOTS, "second")
        for copy in self.made[b]["near"]:
            copy.start()

    def b(self, b):
        _, _, wide, cut, _ = BLOCKS[b]
        m = self.made[b]
        slot = b % C_SLOTS
        for k, (first, last) in enumerate(((0, cut), (cut, wide))):
            m["first"][k].wait_recv()
            m["near"][k].wait()
            self.cs[slot, :, :, first:last] = (
                self.cs[slot, :, :, first:last] + self.r1[2 * b + k][...]
            )
            m["second"][k].start()

    def c0(self, b):
        if b >= H_SLOTS:
            self.settle(b - H_SLOTS, "third", "fourth")
        m = self.made[b]
        for copy in m["first"][2:] + m["second"]:
            copy.wait_recv()
        for copy in m["back"]:
            copy.start()

    def c(self, b):
        wide = BLOCKS[b][2]
        m = self.made[b]
        for copy in m["back"]:
            copy.wait()
        slot, side = b % H_SLOTS, b % L_SLOTS
        total = self.hs[slot, :, :, 0:wide] + (
            self.ls[side, :, :, 0:wide] + self.rs[side, :, :, 0:wide]
        )
        self.hs[slot, :, :, 0:wide] = total
        for copy in m["third"]:
            copy.start()

    def d(self, b):
        _, _, wide, cut, axis = BLOCKS[b]
        m = self.made[b]
        me2 = self.near["x" if axis == "y" else "y"][2]
        slot = b % H_SLOTS
        for k, (by, first, last) in enumerate(((1, 0, cut), (-1, cut, wide))):
            t = self.turn(me2, by)
            m["third"][k].wait_recv()
            self.hs[slot, t, :, first:last] = (
                self.hs[slot, t, :, first:last] + self.second[5 * b + k][...]
            )
            m["fourth"][k].start()

    def e(self, b):
        _, _, wide, _, axis = BLOCKS[b]
        m = self.made[b]
        me2 = self.near["x" if axis == "y" else "y"][2]
        t2l, t2r, zz = self.second[5 * b + 2:5 * b + 5]
        for copy in m["third"][2:] + m["fourth"]:
            copy.wait_recv()
        total = self.hs[b % H_SLOTS, me2, :, 0:wide] + (t2l[...] + t2r[...])
        zz[0:PIECE] = total
        m["fifth"][0].start()

    def f(self, b):
        part, col, wide, _, _ = BLOCKS[b]
        self.made[b]["fifth"][0].wait_recv()
        zz = self.second[5 * b + 4]
        mine = zz[0:PIECE].astype(F32)
        theirs = zz[PIECE:PIECE + 48].astype(F32)
        self.outs[part][:, col:col + wide] = jnp.where(
            self.z == 0, mine[0:40] + theirs[0:40], mine[40:80] + theirs[8:48]
        )

    def finish(self):
        for b in range(COUNT):
            self.settle(b, "first", "second", "third", "fourth", "fifth")

    def run(self, *words):
        for word in words:
            self.steps[word[:-1]](int(word[-1]))


def layer_kernel(
    x_ref, cot_ref, ga_ref, gf_ref,
    wq_in, wk_in, wv_in, wo_in, cos_in, sin_in, turn_in, wg_in, wu_in, wd_in, place_in,
    act_ref, ig_ref, g0, g1, g2, g3, r2l, r2r, o0, o1, o2, o3,
    *scratch,
):
    (
        wq_ref, wk_ref, wv_ref, wo_ref, cos_ref, sin_ref, turn_ref, wd_ref, place_ref,
        hin, gin, normed, qs, ks, vs, probs, mixed, middle, ffn_in, gates, ups, hidden,
        qkv_back, gain_acc, xt, middle_back, snd_a, rcv_a, snd_b, rcv_b, g_stage, cs,
    ) = scratch[:32]
    r1 = scratch[32:32 + 2 * COUNT]
    stage2 = scratch[32 + 2 * COUNT:32 + 7 * COUNT]
    (
        load_sem, in_sem, in_send, ar_send, ar_recv, step_send, step_recv, out_sem, out_send, g_sem,
        ring_send, ring_recv, ring_here,
    ) = scratch[32 + 7 * COUNT:]
    section = lax.axis_index("section")
    shard = lax.axis_index("shard")
    rep = lax.axis_index("replica")
    zlo = lax.rem(lax.div(rep, RING), 2)
    side = rep + RING - 2 * RING * zlo
    core = {"section": 1 - section}
    twin = {"shard": 1 - shard, "replica": side}
    swap = {"replica": side}

    def make_ring(hs, ls, rs):
        return Ring(
            (g0, g1, g2, g3), (o0, o1, o2, o3), r2l, r2r, r1, cs, hs, ls, rs, stage2,
            ring_send, ring_recv, ring_here,
        )

    ring = make_ring(None, None, None)
    wide_weights = []

    loads = [
        pltpu.make_async_copy(source, target, load_sem.at[k])
        for k, (source, target) in enumerate(
            (
                (wq_in, wq_ref), (wk_in, wk_ref), (wv_in, wv_ref), (cos_in, cos_ref),
                (sin_in, sin_ref), (turn_in, turn_ref), (wo_in, wo_ref), (wd_in, wd_ref),
                (place_in, place_ref),
            )
        )
    ]
    for copy in loads[:7]:
        copy.start()

    barrier = pltpu.get_barrier_semaphore()
    near = (core, twin, swap) + ring.neighbours()
    for target in near:
        pl.semaphore_signal(barrier, inc=1, device_id=target, device_id_type=MESH)
    pl.semaphore_wait(barrier, len(near))

    inputs = ((x_ref, hin), (cot_ref, gin))

    def fetch(s, m):
        source, target = inputs[s]
        rows = rows_of(m, 1)

        def local():
            return pltpu.make_async_copy(source.at[m], target.at[rows], in_sem.at[s, m])

        def push():
            return pltpu.make_async_remote_copy(
                source.at[m], target.at[rows], in_send.at[s, m], in_sem.at[s, m],
                device_id=swap, device_id_type=MESH,
            )

        return local, push

    for m in range(SEQS):
        for s in range(2):
            local, push = fetch(s, m)

            @pl.when((section == s) & (shard == 0))
            def _():
                local().start()

            @pl.when((section == s) & (shard == 1))
            def _():
                push().start()

    for copy in loads[7:]:
        copy.start()

    def wait_input(s, m):
        local, push = fetch(s, m)

        @pl.when(shard == 0)
        def _():
            local().wait()

        @pl.when(shard == 1)
        def _():
            push().wait_recv()

    def pass_on(which, first, count, k):
        source, target = ((snd_b, hin), (snd_a, gin))[which]
        rows = rows_of(first, count)
        return pltpu.make_async_remote_copy(
            source.at[rows], target.at[rows], step_send.at[which, k], step_recv.at[which, k],
            device_id=core, device_id_type=MESH,
        )

    halves = ((snd_a, rcv_a), (snd_b, rcv_b), (snd_b, rcv_b), (snd_a, rcv_a))

    def exchange(phase, first, count, k):
        snd, rcv = halves[phase]
        rows = rows_of(first, count)
        return pltpu.make_async_remote_copy(
            snd.at[rows], rcv.at[rows], ar_send.at[phase, k], ar_recv.at[phase, k],
            device_id=twin, device_id_type=MESH,
        )

    def offer(phase, first, count, k, value):
        halves[phase][0][rows_of(first, count), :] = value.astype(BF16)
        exchange(phase, first, count, k).start()

    def exchanged(phase, first, count, k):
        exchange(phase, first, count, k).wait()
        snd, rcv = halves[phase]
        rows = rows_of(first, count)
        return snd[rows, :].astype(F32) + rcv[rows, :].astype(F32)

    def emit(which, m):
        source, target = ((snd_b, act_ref), (snd_a, ig_ref))[which]
        rows = rows_of(m, 1)

        def local():
            return pltpu.make_async_copy(source.at[rows], target.at[m], out_sem.at[which, m])

        def push():
            return pltpu.make_async_remote_copy(
                source.at[rows], target.at[m], out_send.at[which, m], out_sem.at[which, m],
                device_id=swap, device_id_type=MESH,
            )

        return local, push

    def start_emit(which, m):
        local, push = emit(which, m)

        @pl.when(shard == 0)
        def _():
            local().start()

        @pl.when(shard == 1)
        def _():
            push().start()

    def settle_emit(which, m):
        local, push = emit(which, m)

        @pl.when(shard == 0)
        def _():
            local().wait()

        @pl.when(shard == 1)
        def _():
            push().wait_send()

    gain_acc[...] = jnp.zeros_like(gain_acc)
    mixed[:, QW:] = jnp.zeros((TOKENS, 64), BF16)
    qkv_back[:, QW + 2 * KW:] = jnp.zeros((TOKENS, 64), BF16)

    def stacked(value, g):
        return jnp.concatenate(
            [value[:, (3 * g + j) * HEAD:(3 * g + j + 1) * HEAD] for j in range(3)], axis=0
        )

    def turned(value):
        wide = value.shape[1]
        return jnp.concatenate(
            [
                dot(value[:, c:min(c + 128, wide)], turn_ref[:min(128, wide - c), :min(128, wide - c)])
                for c in range(0, wide, 128)
            ],
            axis=1,
        )

    def spread(table, wide):
        return jnp.concatenate(
            [table[:, :min(128, wide - c)] for c in range(0, wide, 128)], axis=1
        )

    def rope(value):
        high = value.astype(BF16)
        low = (value - high.astype(F32)).astype(BF16)
        wide = value.shape[1]
        cosine, sine = spread(cos_ref[...], wide), spread(sin_ref[...], wide)
        return (value * cosine + (turned(high) + turned(low)) * sine).astype(BF16)

    def attention(m):
        rows = rows_of(m, 1)

        @pl.when(section == 0)
        def _():
            wait_input(0, m)

        @pl.when(section == 1)
        def _():
            pass_on(0, m, 1, m).wait_recv()

        h = hin[rows, :].astype(F32)
        normal = (h * rms_factor(h) * ga_ref[...]).astype(BF16)
        normed[rows, :] = normal
        query = rope(dot_nt(normal, wq_ref[...]))
        key = rope(dot_nt(normal, wk_ref[...]))
        value = dot_nt(normal, wv_ref[...]).astype(BF16)
        qs[rows, :] = query
        ks[rows, :] = key
        vs[rows, :] = value
        at = lax.rem(lax.broadcasted_iota(jnp.int32, (3 * LEN, LEN), 0), LEN)
        causal = at >= lax.broadcasted_iota(jnp.int32, (3 * LEN, LEN), 1)
        heads = []
        for g in range(GROUPS):
            cols = slice(g * HEAD, (g + 1) * HEAD)
            scores = dot_nt(stacked(query, g), key[:, cols]) * HEAD**-0.5
            scores = jnp.where(causal, scores, -1e30)
            top = jnp.max(scores, axis=-1, keepdims=True)
            weight = jnp.exp(scores - top)
            prob = (weight / jnp.sum(weight, axis=-1, keepdims=True)).astype(BF16)
            probs[m, g] = prob
            out = dot(prob, value[:, cols]).astype(BF16)
            heads += [out[j * LEN:(j + 1) * LEN] for j in range(3)]
        mix = jnp.concatenate(heads, axis=1)
        mixed[rows, :QW] = mix
        offer(0, m, 1, m, dot(mix, wo_ref[...]))

    def feed_forward(m):
        rows = rows_of(m, 1)
        mid = hin[rows, :].astype(F32) + exchanged(0, m, 1, m)
        middle[rows, :] = mid
        normal = (mid * rms_factor(mid) * gf_ref[...]).astype(BF16)
        ffn_in[rows, :] = normal
        for j in range(0, FF, 512):
            cols = slice(j, j + 512)
            gate = dot(normal, wide_weights[0][:, cols])
            up = dot(normal, wide_weights[1][:, cols])
            gates[rows, cols] = gate.astype(BF16)
            ups[rows, cols] = up.astype(BF16)
            hidden[rows, cols] = (gate * jax.nn.sigmoid(gate) * up).astype(BF16)

        @pl.when(section == 0)
        def _():
            offer(1, m, 1, m, dot(hidden[rows, :], wd_ref[...]))

    def finish(first, count, k):
        value = exchanged(1, first, count, k)
        rows = rows_of(first, count)
        snd_b[rows, :] = (middle[rows, :] + value).astype(BF16)

    def feed_forward_back(j):
        rows = rows_of(2 * j, 2)

        @pl.when(section == 1)
        def _():
            wait_input(1, 2 * j)
            wait_input(1, 2 * j + 1)

        @pl.when(section == 0)
        def _():
            for m in (2 * j, 2 * j + 1):
                pass_on(1, m, 1, m).wait_recv()

        down_in = gin[rows, :]
        total = jnp.zeros((2 * LEN, WIDTH), F32)
        for c in range(0, FF, 512):
            cols = slice(c, c + 512)
            back = dot_nt(down_in, wd_ref[cols, :])
            gate = gates[rows, cols].astype(F32)
            up = ups[rows, cols].astype(F32)
            sig = jax.nn.sigmoid(gate)
            gate_back = (back * up * sig * (1.0 + gate * (1.0 - sig))).astype(BF16)
            up_back = (back * gate * sig).astype(BF16)
            gates[rows, cols] = gate_back
            ups[rows, cols] = up_back
            total += dot_nt(gate_back, wide_weights[0][:, cols]) + dot_nt(up_back, wide_weights[1][:, cols])
        for i in range(2):
            offer(2, 2 * j + i, 1, 2 * j + i, total[i * LEN:(i + 1) * LEN])

    def attention_back(m):
        rows = rows_of(m, 1)
        back = exchanged(2, m, 1, m)
        mid = middle[rows, :]
        factor = rms_factor(mid)
        gain_acc[0:1, :] += jnp.sum(back * mid * factor, axis=0, keepdims=True)
        mid_back = gin[rows, :].astype(F32) + norm_back(mid, factor, back * gf_ref[...])
        middle_back[rows, :] = mid_back
        mixed_back = dot_nt(mid_back.astype(BF16), wo_ref[...]).astype(BF16)
        cosine, sine = cos_ref[:, :HEAD], sin_ref[:, :HEAD]
        query, key, value = qs[rows, :], ks[rows, :], vs[rows, :]
        query_turn = turned(query).astype(BF16)
        key_turn = turned(key).astype(BF16)
        query_out, key_out, value_out = [], [], []
        for g in range(GROUPS):
            cols = slice(g * HEAD, (g + 1) * HEAD)
            prob = probs[m, g]
            prob_f = prob.astype(F32)
            out_back = stacked(mixed_back, g)
            value_out.append(dot_tn(prob, out_back).astype(BF16))
            prob_back = dot_nt(out_back, value[:, cols])
            score_back = (
                prob_f * (prob_back - jnp.sum(prob_back * prob_f, axis=-1, keepdims=True))
            ).astype(BF16)
            both = jnp.concatenate([key[:, cols], key_turn[:, cols]], axis=1)
            both_back = dot(score_back, both) * HEAD**-0.5
            for t in range(3):
                one = both_back[t * LEN:(t + 1) * LEN]
                query_out.append((one[:, :HEAD] * cosine - one[:, HEAD:] * sine).astype(BF16))
            both = jnp.concatenate([stacked(query, g), stacked(query_turn, g)], axis=1)
            one = dot_tn(score_back, both) * HEAD**-0.5
            key_out.append((one[:, :HEAD] * cosine - one[:, HEAD:] * sine).astype(BF16))
        qkv_back[rows, :QW + 2 * KW] = jnp.concatenate(query_out + key_out + value_out, axis=1)
        offer(
            3, m, 1, m,
            dot(qkv_back[rows, :QW], wq_ref[...])
            + dot(qkv_back[rows, QW:QW + KW], wk_ref[...])
            + dot(qkv_back[rows, QW + KW:QW + 2 * KW], wv_ref[...]),
        )

    def finish_back(m):
        rows = rows_of(m, 1)
        back = exchanged(3, m, 1, m)
        h = hin[rows, :].astype(F32)
        factor = rms_factor(h)
        gain_acc[1:2, :] += jnp.sum(back * h * factor, axis=0, keepdims=True)
        snd_a[rows, :] = (
            middle_back[rows, :] + norm_back(h, factor, back * ga_ref[...])
        ).astype(BF16)

        @pl.when(section == 1)
        def _():
            pass_on(1, m, 1, m).start()

        start_emit(1, m)

    def flush(out, slot, half, col, wide):
        return pltpu.make_async_copy(
            g_stage.at[slot, :, :, :, pl.ds(0, wide)],
            out.at[pl.ds(2 * half, 2), :, :, pl.ds(col, wide)],
            g_sem.at[slot],
        )

    def product(right, right_col, out, col, count):
        def step(k, carry):
            slot, half = lax.rem(k, G_SLOTS), lax.rem(k, 2)

            @pl.when(k >= G_SLOTS)
            def _():
                flush(out, slot, half, 0, 512).wait()

            start = pl.multiple_of(lax.div(k, 2) * 512, 512)
            left = xt[pl.ds(pl.multiple_of(half * 640, 640), 640), :]
            g_stage[slot] = (
                dot(left, right[:, pl.ds(right_col + start, 512)])
                .astype(BF16)
                .reshape(2, RING, PIECE, 512)
            )
            flush(out, slot, half, pl.multiple_of(col + start, 128), 512).start()
            return carry

        lax.fori_loop(0, 2 * count, step, 0)
        for k in range(max(0, 2 * count - G_SLOTS), 2 * count):
            flush(out, k % G_SLOTS, k % 2, 0, 512).wait()

    def features(source):
        for c in range(0, TOKENS, 256):
            block = slice(c, c + 256)
            xt[:, block] = dot_nt(place_ref[...], source[block, :].astype(BF16)).astype(BF16)

    def down_gradient(_):
        features(gin)
        product(hidden, 0, g0, 0, 3)
        ring.run("a0", "a1")

    def gate_gradient(_):
        features(ffn_in)
        product(gates, 0, g1, 0, 3)
        ring.run("a2", "a3", "b00", "b01")
        product(ups, 0, g2, 0, 3)
        ring.run("a4", "a5")

    def out_gradient():
        features(middle_back)
        product(mixed, 0, g3, 0, 1)
        gains = jnp.concatenate(
            [jnp.zeros((64, WIDTH), F32), gain_acc[...], jnp.zeros((56, WIDTH), F32)], axis=0
        ).astype(BF16)
        last = (dot(xt[...], mixed[:, 512:640]) + dot_nt(place_ref[...], gains)).astype(BF16)
        for half in range(2):
            g_stage[half, :, :, :, 0:128] = last[half * 640:half * 640 + 640].reshape(
                2, RING, PIECE, 128
            )
            flush(g3, half, half, 512, 128).start()
        for half in range(2):
            flush(g3, half, half, 512, 128).wait()

    def plan(t, ours, theirs):
        index = jnp.int32(-1)
        for k, (one, other) in enumerate(zip(ours, theirs)):
            if one >= 0 or other >= 0:
                index = jnp.where(t == k, jnp.where(section == 0, one, other), index)
        return index

    def tick(t, carry):
        def do(work, ours, theirs):
            index = plan(t, ours, theirs)

            @pl.when(index >= 0)
            def _():
                work(index)

        def finish_forward(m):
            finish(m, 1, m)
            pass_on(0, m, 1, m).start()
            start_emit(0, m)

        @pl.when(t == 1)
        def _():
            for copy in loads[7:] + wide_loads:
                copy.wait()

        do(
            attention,
            (0, 1, 2, -1, 3, -1, -1, -1, -1, -1, -1, -1, -1, -1),
            (0, 1, 2, -1, -1, 3, -1, -1, -1, -1, -1, -1, -1, -1),
        )
        do(
            finish_forward,
            (-1, -1, -1, -1, 0, 1, 2, 3, -1, -1, -1, -1, -1, -1),
            (-1, -1, -1, -1, -1, -1, -1, -1, -1, -1, -1, -1, -1, -1),
        )
        do(
            feed_forward,
            (-1, -1, 0, 1, 2, 3, -1, -1, -1, -1, -1, -1, -1, -1),
            (-1, -1, 0, 1, 2, -1, -1, 3, -1, -1, -1, -1, -1, -1),
        )

        @pl.when((t == 7) & (section == 0))
        def _():
            for m in range(SEQS):
                pass_on(0, m, 1, m).wait_send()
                settle_emit(0, m)

        do(
            finish_back,
            (-1,) * 14,
            (-1, -1, -1, -1, -1, -1, -1, 0, 1, -1, -1, 2, 3, -1),
        )
        do(
            feed_forward_back,
            (-1, -1, -1, -1, -1, -1, -1, 0, -1, 1, -1, -1, -1, -1),
            (-1, -1, -1, 0, -1, -1, -1, 1, -1, -1, -1, -1, -1, -1),
        )
        do(
            down_gradient,
            (-1, -1, -1, -1, -1, -1, -1, -1, -1, 0, -1, -1, -1, -1),
            (-1, -1, -1, -1, -1, -1, -1, -1, 0, -1, -1, -1, -1, -1),
        )
        do(
            gate_gradient,
            (-1, -1, -1, -1, -1, -1, -1, -1, -1, 0, -1, -1, -1, -1),
            (-1, -1, -1, -1, -1, -1, -1, -1, -1, -1, 0, -1, -1, -1),
        )
        do(
            attention_back,
            (-1, -1, -1, -1, -1, -1, -1, 0, 1, 2, 3, -1, -1, -1),
            (-1, -1, -1, -1, -1, 0, 1, -1, 2, 3, -1, -1, -1, -1),
        )
        return carry

    wide_loads = []

    def first_phase(wg_ref, wu_ref):
        wide_weights[:] = [wg_ref, wu_ref]
        wide_loads[:] = [
            pltpu.make_async_copy(wg_in, wg_ref, load_sem.at[9]),
            pltpu.make_async_copy(wu_in, wu_ref, load_sem.at[10]),
        ]
        for copy in wide_loads:
            copy.start()
        for copy in loads[:7]:
            copy.wait()
        lax.fori_loop(0, 14, tick, 0)

    pl.run_scoped(first_phase, pltpu.VMEM((WIDTH, FF), BF16), pltpu.VMEM((WIDTH, FF), BF16))

    def second_phase(hs, ls, rs):
        steps = make_ring(hs, ls, rs)
        steps.run("b0", "b1")

        @pl.when(section == 1)
        def _():
            for j in range(2):
                offer(1, 2 * j, 2, j, dot(hidden[rows_of(2 * j, 2), :], wd_ref[...]))

        steps.run("b02", "b03")
        features(normed)
        product(qkv_back, 0, g3, 640, 1)
        steps.run("a7", "b2", "b3", "b04", "b05")
        product(qkv_back, 512, g3, 1152, 1)
        steps.run("a8", "a9")

        @pl.when(section == 0)
        def _():
            def late_finish(m, carry):
                finish_back(m)
                return carry

            lax.fori_loop(0, SEQS, late_finish, 0)

        out_gradient()
        steps.run(
            "a6", "c00", "c01", "c02", "c03", "b4", "b5", "b06", "b07", "b08", "b09",
            "c0", "c1", "c2", "c3", "b6", "b7", "b8", "b9", "d0", "d1", "c04", "c4",
            "d2", "d3", "e0", "e1", "c05", "c06", "c5", "c6", "e2", "e3", "f0", "f1",
        )

        @pl.when(section == 1)
        def _():
            for j in range(2):
                finish(2 * j, 2, j)
                start_emit(0, 2 * j)
                start_emit(0, 2 * j + 1)

        steps.run(
            "c07", "c08", "c7", "c8", "d4", "d5", "e4", "c09", "d6", "e5", "c9", "d7",
            "d8", "f2", "f3", "d9", "e6", "e7", "e8", "e9", "f4", "f5", "f6", "f7",
            "f8", "f9",
        )
        steps.finish()

    pl.run_scoped(
        second_phase,
        *[
            pltpu.VMEM((slots, RING, PIECE, WIDE), BF16)
            for slots in (H_SLOTS, L_SLOTS, L_SLOTS)
        ],
    )

    for m in range(SEQS):
        for s in range(2):
            @pl.when((section == s) & (shard == 1))
            def _():
                fetch(s, m)[1]().wait_send()

        @pl.when(section == 1)
        def _():
            settle_emit(0, m)

        settle_emit(1, m)

        @pl.when(shard == 1)
        def _():
            for which in range(2):
                emit(which, m)[1]().wait_recv()

    for j in range(SEQS):
        @pl.when(section == 1)
        def _():
            pass_on(1, j, 1, j).wait_send()


def deliver_kernel(
    act_in, ig_in, down, gate, up, mix,
    act, ig, gain_a, query, key, value, out, gain_f, gate_out, up_out, down_out,
):
    act[...] = act_in[...]
    ig[...] = ig_in[...]
    for target, source, first, wide in (
        (query, mix, 640, QW),
        (key, mix, 640 + QW, KW),
        (value, mix, 640 + QW + KW, KW),
        (out, mix, 0, QW),
        (gate_out, gate, 0, FF),
        (up_out, up, 0, FF),
        (down_out, down, 0, FF),
    ):
        target[...] = source[0:OWN, first:first + wide].reshape(OWN, 1, wide)
    gains = mix[:, 512:640].T
    gain_f[...] = gains[64:65, 0:OWN]
    gain_a[...] = gains[65:66, 0:OWN]


def on_device(x, cot, ga, wq, wk, wv, wo, gf, wg, wu, wd):
    cosine, sine = rope_tables()
    vmem = pl.BlockSpec(memory_space=pltpu.VMEM)
    any_ = pl.BlockSpec(memory_space=pl.ANY)
    sds = jax.ShapeDtypeStruct
    rows = (TOKENS, WIDTH)
    dma = pltpu.SemaphoreType.DMA
    operands = (
        wq[0].T, wk[0].T, wv[0].T, wo[0], jnp.asarray(cosine), jnp.asarray(sine),
        jnp.asarray(turn_matrix(), BF16), wg[0], wu[0], wd[0], jnp.asarray(place_matrix(), BF16),
    )

    def buffer(shape, kind=BF16):
        return pltpu.VMEM(shape, kind)

    scratch = [
        buffer(item.shape, item.dtype) for k, item in enumerate(operands) if k not in (7, 8)
    ]
    scratch += [buffer(rows)] * 3
    scratch += [
        buffer((TOKENS, QW)),
        buffer((TOKENS, KW)),
        buffer((TOKENS, KW)),
        buffer((SEQS, GROUPS, 3 * LEN, LEN)),
        buffer((TOKENS, 640)),
        buffer(rows, F32),
        buffer(rows),
        buffer((TOKENS, FF)),
        buffer((TOKENS, FF)),
        buffer((TOKENS, FF)),
        buffer((TOKENS, 1024)),
        buffer((8, WIDTH), F32),
        buffer((ROWS, TOKENS)),
        buffer(rows, F32),
    ]
    scratch += [buffer(rows)] * 4
    scratch += [
        buffer((G_SLOTS, 2, RING, PIECE, 512)),
        buffer((C_SLOTS, RING, PIECE, WIDE)),
    ]
    for _, _, wide, cut, _ in BLOCKS:
        scratch += [buffer((RING, PIECE, cut)), buffer((RING, PIECE, wide - cut))]
    for _, _, wide, cut, _ in BLOCKS:
        scratch += [
            buffer((PIECE, cut)),
            buffer((PIECE, wide - cut)),
            buffer((PIECE, wide)),
            buffer((PIECE, wide)),
            buffer((PIECE + 48, wide)),
        ]
    scratch += [
        dma((len(operands),)),
        dma((2, SEQS)),
        dma((2, SEQS)),
        dma((4, SEQS)),
        dma((4, SEQS)),
        dma((2, SEQS)),
        dma((2, SEQS)),
        dma((2, SEQS)),
        dma((2, SEQS)),
        dma((G_SLOTS,)),
        dma((COUNT, 13)),
        dma((COUNT, 13)),
        dma((COUNT, 5)),
    ]
    outs = pl.pallas_call(
        layer_kernel,
        out_shape=(
            [sds(x.shape, BF16)] * 2
            + [sds((RING, RING, PIECE, columns), BF16) for columns in PARTS]
            + [sds((RING, PIECE, COLUMNS), BF16)] * 2
            + [sds((40, columns), F32) for columns in PARTS]
        ),
        in_specs=[any_] * 2 + [vmem] * 2 + [any_] * len(operands),
        out_specs=[any_] * 8 + [vmem] * 4,
        scratch_shapes=scratch,
        compiler_params=pltpu.CompilerParams(
            collective_id=0, has_side_effects=True, vmem_limit_bytes=63 * 2**20
        ),
        cost_estimate=pl.CostEstimate(
            flops=26 * 10**9, bytes_accessed=60 * 10**6, transcendentals=10**7
        ),
        name="layer",
    )(x, cot, ga, gf, *operands)
    acts, grads = outs[:2]
    done = pl.pallas_call(
        deliver_kernel,
        out_shape=(
            [sds(x.shape, BF16)] * 2
            + [sds((1, OWN), F32)]
            + [sds((OWN, 1, wide), F32) for wide in (QW, KW, KW, QW)]
            + [sds((1, OWN), F32)]
            + [sds((OWN, 1, FF), F32)] * 3
        ),
        in_specs=[vmem] * 6,
        out_specs=[vmem] * 11,
        name="deliver",
    )(acts, grads, *outs[8:])
    act, ig, gain_a, query, key, value, out, gain_f, gate, up, down = done

    def rows_out(item):
        return item.transpose(1, 0, 2)

    def columns_out(item):
        return item.transpose(1, 2, 0)

    return (
        act[None], ig[None], gain_a, rows_out(query), rows_out(key), rows_out(value),
        columns_out(out), gain_f, rows_out(gate), rows_out(up), columns_out(down),
    )


def solution(mesh):
    in_specs = (
        P("replica", None, None),
        P("replica", None, None),
        P("section", None),
        P("section", None, "shard"),
        P("section", None, "shard"),
        P("section", None, "shard"),
        P("section", "shard", None),
        P("section", None),
        P("section", None, "shard"),
        P("section", None, "shard"),
        P("section", "shard", None),
    )
    out_specs = (
        P("section", "replica", None, None),
        P("section", "replica", None, None),
        P("section", "replica"),
        P("section", "replica", "shard"),
        P("section", "replica", "shard"),
        P("section", "replica", "shard"),
        P("section", "shard", "replica"),
        P("section", "replica"),
        P("section", "replica", "shard"),
        P("section", "replica", "shard"),
        P("section", "shard", "replica"),
    )
    return jax.shard_map(
        on_device, mesh=mesh, in_specs=in_specs, out_specs=out_specs, check_vma=False
    )
```
